32 devices in a mesh: island: 8 (over y, x, core), fsdp: 4 (over z).
Axes of the slice: x: 2, y: 2, z: 4, core: 2. Of those that a mesh axis runs over, the one named last changes fastest.
Arguments:
- tokens: bfloat16 [16384, 2048], P(('island', 'fsdp')), may hold values from -6 to 6
- cotangent: bfloat16 [16384, 2048], P(('island', 'fsdp')), may hold values from -0.125 to 0.125
- norm_gain: float32 [8, 2048], P('island'), may hold values from 0.5 to 1.5
- qkv_weight: bfloat16 [8, 2048, 1536], P('island', 'fsdp'), may hold values from -0.125 to 0.125
- out_weight: bfloat16 [8, 1024, 2048], P('island', 'fsdp'), may hold values from -0.1875 to 0.1875
- gain_first: float32 [8, 2048], P('island'), may hold values from -2 to 2
- gain_second: float32 [8, 2048], P('island'), may hold values from 0.01 to 1
- qkv_first: float32 [8, 2048, 1536], P('island', 'fsdp'), may hold values from -2 to 2
- qkv_second: float32 [8, 2048, 1536], P('island', 'fsdp'), may hold values from 0.01 to 1
- out_first: float32 [8, 1024, 2048], P('island', 'fsdp'), may hold values from -2 to 2
- out_second: float32 [8, 1024, 2048], P('island', 'fsdp'), may hold values from 0.01 to 1
- gain_global: float32 [2048], replicated, may hold values from 0.5 to 1.5
- gain_momentum: float32 [2048], replicated, may hold values from -1 to 1
- qkv_global: float32 [2048, 1536], P('fsdp', 'island'), may hold values from -0.125 to 0.125
- qkv_momentum: float32 [2048, 1536], P('fsdp', 'island'), may hold values from -0.1 to 0.1
- out_global: float32 [1024, 2048], P('fsdp', 'island'), may hold values from -0.1875 to 0.1875
- out_momentum: float32 [1024, 2048], P('fsdp', 'island'), may hold values from -0.1 to 0.1
Outputs:
- gain_next: float32 [8, 2048], P('island')
- qkv_next: bfloat16 [8, 2048, 1536], P('island', 'fsdp')
- out_next: bfloat16 [8, 1024, 2048], P('island', 'fsdp')
- gain_first_next: float32 [8, 2048], P('island')
- gain_second_next: float32 [8, 2048], P('island')
- qkv_first_next: float32 [8, 2048, 1536], P('island', 'fsdp')
- qkv_second_next: float32 [8, 2048, 1536], P('island', 'fsdp')
- out_first_next: float32 [8, 1024, 2048], P('island', 'fsdp')
- out_second_next: float32 [8, 1024, 2048], P('island', 'fsdp')
- gain_global_next: float32 [2048], replicated
- gain_momentum_next: float32 [2048], replicated
- qkv_global_next: float32 [2048, 1536], P('fsdp', 'island')
- qkv_momentum_next: float32 [2048, 1536], P('fsdp', 'island')
- out_global_next: float32 [1024, 2048], P('fsdp', 'island')
- out_momentum_next: float32 [1024, 2048], P('fsdp', 'island')
The draws below stay inside these ranges and needn't reach their ends.
All inputs are finite; a program needn't handle non-finite values.
Results may differ from the reference program's by a relative error of at most 0.01.
Values may be sent and summed in bfloat16 or wider, within the bound.
No kernel may reach another device: no remote copies, remote signals or barrier semaphores. Data moves between devices by JAX's collectives and lax.ppermute only.
A program may use at most 192 MiB of HBM per device.

```python
import math
import jax
import jax.numpy as jnp
from jax import lax

D = 2048
HEADS = 16
KV_HEADS = 4
HEAD_DIM = 64
TOK_DEV = 512
QW = 1024
QKV = 1536
ISLANDS = 8
TOKENS = 16384
N_ISLAND = 8
N_FSDP = 4


def block_levels(stream_key, extent, shards, least, largest):
    level = 1.0
    for axis_at, parts in shards:
        heights = jax.random.uniform(jax.random.fold_in(jax.random.fold_in(stream_key, 6), axis_at), (parts,), jnp.float32, least / len(shards), largest / len(shards))
        level = level * jnp.repeat(jnp.exp(heights), extent[axis_at] // parts).reshape((-1,) + (1,) * (len(extent) - 1 - axis_at))
    return level


def scatter_about(rng, extent, width, limit, cuts=(), held_as=jnp.bfloat16):
    factor_of = block_levels(rng, extent, cuts, -0.22, 0.18) if cuts else 1.0
    array = jax.random.normal(rng, extent, jnp.float32) * width * factor_of
    return jnp.minimum(jnp.maximum(array, -limit), limit).astype(held_as)


def setup_inputs(seed: int = 0) -> dict:
    splits = jax.random.split(jax.random.key(seed), 18)
    return {
        "tokens": scatter_about(splits[0], (TOKENS, D), 1.0, 6.0, ((0, 32),)),
        "cotangent": scatter_about(splits[1], (TOKENS, D), (TOK_DEV * N_FSDP) ** -0.5, 0.125, ((0, 32),)),
        "norm_gain": jnp.clip(1.0 + 0.1 * jax.random.normal(splits[2], (ISLANDS, D), jnp.float32), 0.5, 1.5),
        "qkv_weight": scatter_about(splits[3], (ISLANDS, D, QKV), D ** -0.5, 0.125, ((0, 8), (1, 4))),
        "out_weight": scatter_about(splits[4], (ISLANDS, QW, D), QW ** -0.5, 0.1875, ((0, 8), (1, 4))),
        "gain_first": scatter_about(splits[5], (ISLANDS, D), 0.3, 2.0, ((0, 8),), jnp.float32),
        "gain_second": jnp.clip(jnp.exp(math.log(1.0) - 4.6051702 * jax.random.uniform(splits[6], (ISLANDS, D), jnp.float32) ** block_levels(splits[6], (ISLANDS, D), ((0, 8),), -0.2, 0.2)), 0.01, 1.0),
        "qkv_first": scatter_about(splits[7], (ISLANDS, D, QKV), 0.3, 2.0, ((0, 8), (1, 4)), jnp.float32),
        "qkv_second": jnp.clip(jnp.exp(math.log(1.0) - 4.6051702 * jax.random.uniform(splits[8], (ISLANDS, D, QKV), jnp.float32) ** block_levels(splits[8], (ISLANDS, D, QKV), ((0, 8), (1, 4)), -0.2, 0.2)), 0.01, 1.0),
        "out_first": scatter_about(splits[9], (ISLANDS, QW, D), 0.3, 2.0, ((0, 8), (1, 4)), jnp.float32),
        "out_second": jnp.clip(jnp.exp(math.log(1.0) - 4.6051702 * jax.random.uniform(splits[10], (ISLANDS, QW, D), jnp.float32) ** block_levels(splits[10], (ISLANDS, QW, D), ((0, 8), (1, 4)), -0.2, 0.2)), 0.01, 1.0),
        "gain_global": jnp.clip(1.0 + 0.1 * jax.random.normal(splits[11], (D,), jnp.float32), 0.5, 1.5),
        "gain_momentum": scatter_about(splits[12], (D,), 0.1, 1.0, (), jnp.float32),
        "qkv_global": scatter_about(splits[13], (D, QKV), D ** -0.5, 0.125, ((0, 4), (1, 8)), jnp.float32),
        "qkv_momentum": scatter_about(splits[14], (D, QKV), 0.01, 0.1, ((0, 4), (1, 8)), jnp.float32),
        "out_global": scatter_about(splits[15], (QW, D), QW ** -0.5, 0.1875, ((0, 4), (1, 8)), jnp.float32),
        "out_momentum": scatter_about(splits[16], (QW, D), 0.01, 0.1, ((0, 4), (1, 8)), jnp.float32),
    }


BETA_ONE = 0.9
BETA_TWO = 0.95
ADAM_EPS = 1e-08
INNER_RATE = 0.001
WEIGHT_DECAY = 0.1
STEP_COUNT = 100.0
OUTER_RATE = 0.7
OUTER_MOMENTUM = 0.9
MIXING = 0.5
NORM_EPS = 1e-05
ROPE_BASE = 500000.0

def rotary(heads, positions):
    half = heads.shape[-1] // 2
    freqs = ROPE_BASE ** (-jnp.arange(half, dtype=jnp.float32) / half)
    angles = positions[:, None] * freqs[None, :]
    cosine = jnp.cos(angles)[:, None, :]
    sine = jnp.sin(angles)[:, None, :]
    first = heads[..., :half]
    second = heads[..., half:]
    return jnp.concatenate([first * cosine - second * sine, first * sine + second * cosine], axis=-1)

def block_output(seq, gain, wqkv, wout):
    length = seq.shape[0]
    wide = seq.astype(jnp.float32)
    factor = lax.rsqrt(lax.optimization_barrier(jnp.mean(wide * wide, axis=-1, keepdims=True)) + NORM_EPS)
    normed = (wide * factor * gain).astype(jnp.bfloat16)
    mixed = jnp.dot(normed, wqkv, preferred_element_type=jnp.float32)
    qwidth = HEADS * HEAD_DIM
    kwidth = KV_HEADS * HEAD_DIM
    queries = mixed[:, :qwidth].reshape(length, HEADS, HEAD_DIM)
    keys = mixed[:, qwidth:qwidth + kwidth].reshape(length, KV_HEADS, HEAD_DIM)
    values = mixed[:, qwidth + kwidth:].reshape(length, KV_HEADS, HEAD_DIM).astype(jnp.bfloat16)
    positions = jnp.arange(length, dtype=jnp.float32)
    queries = rotary(queries, positions).astype(jnp.bfloat16)
    keys = rotary(keys, positions).astype(jnp.bfloat16)
    queries = queries.reshape(length, KV_HEADS, HEADS // KV_HEADS, HEAD_DIM)
    scores = jnp.einsum('qkgd,skd->kgqs', queries.astype(jnp.float32), keys.astype(jnp.float32)) * HEAD_DIM ** (-0.5)
    causal = positions[:, None] >= positions[None, :]
    scores = jnp.where(causal, scores, -1e+30)
    weights = jax.nn.softmax(scores, axis=-1).astype(jnp.bfloat16)
    attended = jnp.einsum('kgqs,skd->qkgd', weights.astype(jnp.float32), values.astype(jnp.float32))
    attended = attended.astype(jnp.bfloat16).reshape(length, qwidth)
    return jnp.dot(attended, wout, preferred_element_type=jnp.float32)

def sequence_grads(seq, cot, gain, wqkv, wout):

    def loss(gain_in, qkv_in, out_in):
        return jnp.sum(block_output(seq, gain_in, qkv_in, out_in) * cot.astype(jnp.float32))
    return jax.grad(loss, argnums=(0, 1, 2))(gain, wqkv, wout)

def adamw(param, grad, first, second, decay):
    wide = param.astype(jnp.float32)
    first_next = BETA_ONE * first + (1.0 - BETA_ONE) * grad
    second_next = BETA_TWO * second + (1.0 - BETA_TWO) * grad * grad
    update = first_next / (1.0 - BETA_ONE ** STEP_COUNT) / (jnp.sqrt(second_next / (1.0 - BETA_TWO ** STEP_COUNT)) + ADAM_EPS)
    return (wide - INNER_RATE * (update + decay * wide), first_next, second_next)

def nesterov(global_value, momentum, average):
    delta = global_value - average
    momentum_next = OUTER_MOMENTUM * momentum + delta
    return (global_value - OUTER_RATE * (delta + OUTER_MOMENTUM * momentum_next), momentum_next)

def reference(tokens, cotangent, norm_gain, qkv_weight, out_weight, gain_first, gain_second, qkv_first, qkv_second, out_first, out_second, gain_global, gain_momentum, qkv_global, qkv_momentum, out_global, out_momentum):
    seqs = tokens.reshape(N_ISLAND, N_FSDP, TOK_DEV, D)
    cots = cotangent.reshape(N_ISLAND, N_FSDP, TOK_DEV, D)

    def one_island(item):
        island_seqs, island_cots, gain, wqkv, wout = item

        def accumulate(carry, pair):
            g_gain, g_qkv, g_out = sequence_grads(pair[0], pair[1], gain, wqkv, wout)
            return ((carry[0] + g_gain, carry[1] + g_qkv.astype(jnp.float32), carry[2] + g_out.astype(jnp.float32)), None)
        start = (jnp.zeros(gain.shape, jnp.float32), jnp.zeros(wqkv.shape, jnp.float32), jnp.zeros(wout.shape, jnp.float32))
        sums, _ = lax.scan(accumulate, start, (island_seqs, island_cots))
        return sums
    gain_grad, qkv_grad, out_grad = lax.map(one_island, (seqs, cots, norm_gain, qkv_weight, out_weight))
    gain_step, gain_first_next, gain_second_next = adamw(norm_gain, gain_grad, gain_first, gain_second, 0.0)
    qkv_step, qkv_first_next, qkv_second_next = adamw(qkv_weight, qkv_grad, qkv_first, qkv_second, WEIGHT_DECAY)
    out_step, out_first_next, out_second_next = adamw(out_weight, out_grad, out_first, out_second, WEIGHT_DECAY)
    scale = 1.0 / N_ISLAND
    gain_global_next, gain_momentum_next = nesterov(gain_global, gain_momentum, lax.optimization_barrier(jnp.sum(norm_gain, axis=0)) * scale)
    qkv_global_next, qkv_momentum_next = nesterov(qkv_global, qkv_momentum, lax.optimization_barrier(jnp.sum(qkv_weight.astype(jnp.float32), axis=0)) * scale)
    out_global_next, out_momentum_next = nesterov(out_global, out_momentum, lax.optimization_barrier(jnp.sum(out_weight.astype(jnp.float32), axis=0)) * scale)
    gain_next = MIXING * gain_step + (1.0 - MIXING) * gain_global_next[None]
    qkv_next = (MIXING * qkv_step + (1.0 - MIXING) * qkv_global_next[None]).astype(jnp.bfloat16)
    out_next = (MIXING * out_step + (1.0 - MIXING) * out_global_next[None]).astype(jnp.bfloat16)
    return (gain_next, qkv_next, out_next, gain_first_next, gain_second_next, qkv_first_next, qkv_second_next, out_first_next, out_second_next, gain_global_next, gain_momentum_next, qkv_global_next, qkv_momentum_next, out_global_next, out_momentum_next)
```

```python
import functools

import jax
import jax.numpy as jnp
from jax import lax
from jax.experimental import pallas as pl
from jax.experimental.pallas import tpu as pltpu
from jax.sharding import PartitionSpec as P

HEADS = 16
KV_HEADS = 4
HEAD_DIM = 64
GROUP = HEADS // KV_HEADS
QG = GROUP * HEAD_DIM
CG = QG + 2 * HEAD_DIM

BETA_ONE = 0.9
BETA_TWO = 0.95
ADAM_EPS = 1e-08
INNER_RATE = 0.001
WEIGHT_DECAY = 0.1
STEP_COUNT = 100.0
OUTER_RATE = 0.7
OUTER_MOMENTUM = 0.9
MIXING = 0.5
NORM_EPS = 1e-05
ROPE_BASE = 500000.0
VMEM_LIMIT = 50 * 1024 * 1024

ORDER = (1, 0, 3, 2)
F32 = jnp.float32
BF16 = jnp.bfloat16
NN = (((1,), (0,)), ((), ()))
NT = (((1,), (1,)), ((), ()))


def mm(a, b, dims=NN):
    return lax.dot_general(a, b, dims, preferred_element_type=F32)


def rope_tables(length):
    half = HEAD_DIM // 2
    freqs = ROPE_BASE ** (-jnp.arange(half, dtype=F32) / half)
    angles = jnp.arange(length, dtype=F32)[:, None] * freqs[None, :]
    cosine = jnp.cos(angles)
    sine = jnp.sin(angles)
    zero = jnp.zeros_like(sine)
    one = jnp.ones_like(sine)
    c = jnp.concatenate([cosine] * 6 + [one] * 2, axis=1)
    above = jnp.concatenate([zero, sine] * 3 + [zero] * 2, axis=1)
    below = jnp.concatenate([-sine, zero] * 3 + [zero] * 2, axis=1)
    return jnp.stack([c, above, below])


def turn(x, tab, at, sign):
    c = tab[0, :, at : at + 128]
    above = tab[1, :, at : at + 128]
    below = tab[2, :, at : at + 128]
    side = pltpu.roll(x, 32, 1) * above + pltpu.roll(x, 96, 1) * below
    return x * c + sign * side


def group_kernel(spec, idx_ref, normed, normed_t, cot, tab, gain_in, *refs):
    n, q_keys, o_keys, owners = spec
    q_cand = refs[: len(q_keys)]
    o_cand = refs[len(q_keys) : len(q_keys) + len(o_keys)]
    gq_ref, go_ref, gain_ref, wq, wo, q_sem, o_sem = refs[len(q_keys) + len(o_keys) :]
    me = idx_ref[0]
    rows = wq.shape[0] // n
    orows = wo.shape[0] // len(owners)
    plans = []
    for at, delta in enumerate(q_keys):
        src = me - delta
        here = jnp.logical_and(src >= 0, src < n)
        plans.append((here, q_cand[at], wq, src, rows, q_sem.at[at]))
    for at, delta in enumerate(o_keys):
        src = me - delta
        here = jnp.logical_and(src >= owners[0], src <= owners[-1])
        plans.append((here, o_cand[at], wo, src - owners[0], orows, o_sem.at[at]))

    def copy_of(plan):
        _, src_ref, dst, at, size, sem = plan
        start = pl.multiple_of(at * size, size)
        return pltpu.make_async_copy(src_ref, dst.at[pl.ds(start, size)], sem)

    for plan in plans:
        @pl.when(plan[0])
        def _(plan=plan):
            copy_of(plan).start()
    for plan in plans:
        @pl.when(plan[0])
        def _(plan=plan):
            copy_of(plan).wait()

    length = normed.shape[0]
    mixed = mm(normed[...], wq[...])
    datt = mm(cot[...], wo[...], NT).astype(BF16)
    kv = turn(mixed[:, QG:], tab, 128, 1.0).astype(BF16).astype(F32)
    lane = lax.broadcasted_iota(jnp.int32, kv.shape, 1)
    left = lane < HEAD_DIM
    k_left = jnp.where(left, kv, 0.0)
    v_right = jnp.where(left, 0.0, kv)
    keys = (k_left.astype(BF16), pltpu.roll(k_left, HEAD_DIM, 1).astype(BF16))
    values = (pltpu.roll(v_right, HEAD_DIM, 1).astype(BF16), v_right.astype(BF16))

    step = length // 2
    dk_t = [[None] * 2 for _ in range(2)]
    dv_t = [[None] * 2 for _ in range(2)]
    row = lax.broadcasted_iota(jnp.int32, (step, step), 0)
    col = lax.broadcasted_iota(jnp.int32, (step, step), 1)
    causal = row >= col

    def added(total, part):
        return part if total is None else total + part

    att_t = []
    dm = []
    for pair in range(QG // 128):
        qf = turn(mixed[:, pair * 128 : pair * 128 + 128], tab, 0, 1.0).astype(BF16).astype(F32) * HEAD_DIM**-0.5
        q = qf.astype(BF16)
        q_t = qf.T.astype(BF16)
        da = datt[:, pair * 128 : pair * 128 + 128]
        da_t = da.astype(F32).T.astype(BF16)
        att = [None] * 2
        dq = [None] * 2
        for half in range(2):
            key = keys[half]
            value = values[half]
            for blk in range(2):
                r0 = blk * step
                nk = r0 + step
                s = mm(q[r0 : r0 + step], key[:nk], NT)
                last = jnp.where(causal, s[:, r0:], -1e30)
                s = last if blk == 0 else jnp.concatenate([s[:, :r0], last], axis=1)
                top = jnp.max(s, axis=1, keepdims=True)
                e = jnp.exp(s - top)
                p = e * (1.0 / jnp.sum(e, axis=1, keepdims=True))
                pb = p.astype(BF16)
                att[blk] = added(att[blk], mm(pb, value[:nk]))
                dp = mm(da[r0 : r0 + step], value[:nk], NT)
                ds = (p * (dp - jnp.sum(p * dp, axis=1, keepdims=True))).astype(BF16)
                dq[blk] = added(dq[blk], mm(ds, key[:nk]))
                dv = mm(da_t[:, r0 : r0 + step], pb)
                dk = mm(q_t[:, r0 : r0 + step], ds)
                for kb in range(blk + 1):
                    cut = slice(kb * step, kb * step + step)
                    dv_t[half][kb] = added(dv_t[half][kb], dv[:, cut])
                    dk_t[half][kb] = added(dk_t[half][kb], dk[:, cut])
        att = jnp.concatenate(att, axis=0).astype(BF16).astype(F32)
        att_t.append(att.T.astype(BF16))
        dq = jnp.concatenate(dq, axis=0) * HEAD_DIM**-0.5
        dm.append(turn(dq, tab, 0, -1.0).astype(BF16))
    go_ref[...] = mm(jnp.concatenate(att_t, axis=0), cot[...]).astype(BF16)
    d_kv = []
    for kb in range(2):
        dk = dk_t[0][kb][:HEAD_DIM] + dk_t[1][kb][HEAD_DIM:]
        dv = dv_t[0][kb][:HEAD_DIM] + dv_t[1][kb][HEAD_DIM:]
        d_kv.append(jnp.concatenate([dk, dv], axis=0).T)
    dm.append(turn(jnp.concatenate(d_kv, axis=0), tab, 128, -1.0).astype(BF16))
    dm = jnp.concatenate(dm, axis=1)
    ones = jnp.ones((8, CG), BF16)
    block = 512
    for at in range(wq.shape[0] // block):
        cut = slice(at * block, at * block + block)
        g = mm(normed_t[cut, :], dm)
        gq_ref[cut, :] = g.astype(BF16)
        prod = g * wq[cut, :].astype(F32)
        high = prod.astype(BF16)
        low = (prod - high.astype(F32)).astype(BF16)
        gain_ref[:, cut] = gain_in[:, cut] + mm(ones, high, NT) + mm(ones, low, NT)


def group_step(n, owners, idx, normed, normed_t, cot, tab, gain_in, q_cand, o_cand):
    q_keys = tuple(q_cand)
    o_keys = tuple(o_cand)
    width = normed.shape[1]
    orows = o_cand[0].shape[0] * len(owners)
    whole = pl.BlockSpec(memory_space=pltpu.VMEM)
    hbm = pl.BlockSpec(memory_space=pl.ANY)
    return pl.pallas_call(
        functools.partial(group_kernel, (n, q_keys, o_keys, owners)),
        out_shape=(
            jax.ShapeDtypeStruct((width, CG), BF16),
            jax.ShapeDtypeStruct((orows, width), BF16),
            jax.ShapeDtypeStruct((8, width), F32),
        ),
        in_specs=[pl.BlockSpec(memory_space=pltpu.SMEM)] + [whole] * 5 + [hbm] * (len(q_keys) + len(o_keys)),
        out_specs=(whole, whole, whole),
        scratch_shapes=[
            pltpu.VMEM((width, CG), BF16),
            pltpu.VMEM((orows, width), BF16),
            pltpu.SemaphoreType.DMA((len(q_keys),)),
            pltpu.SemaphoreType.DMA((len(o_keys),)),
        ],
        compiler_params=pltpu.CompilerParams(vmem_limit_bytes=VMEM_LIMIT),
        cost_estimate=pl.CostEstimate(flops=4_000_000_000, bytes_accessed=12_000_000, transcendentals=1_000_000),
    )(idx, normed, normed_t, cot, tab, gain_in, *q_cand.values(), *o_cand.values())


def adam(wide, grad, first, second, decay):
    first_next = BETA_ONE * first + (1.0 - BETA_ONE) * grad
    second_next = BETA_TWO * second + (1.0 - BETA_TWO) * grad * grad
    update = (
        first_next
        / (1.0 - BETA_ONE**STEP_COUNT)
        / (jnp.sqrt(second_next / (1.0 - BETA_TWO**STEP_COUNT)) + ADAM_EPS)
    )
    return (wide - INNER_RATE * (update + decay * wide), first_next, second_next)


def mixed_step(w, grad, first, second, outer):
    stepped, first_next, second_next = adam(w.astype(F32), grad, first, second, WEIGHT_DECAY)
    new = (MIXING * stepped + (1.0 - MIXING) * outer.astype(F32)).astype(BF16)
    return new, first_next, second_next


def qkv_adam_kernel(idx_ref, *refs):
    parts = refs[: 3 * KV_HEADS]
    w, first, second, outer, new, first_next, second_next = refs[3 * KV_HEADS :]
    grads = []
    for g in range(KV_HEADS):
        own, down, up = parts[3 * g : 3 * g + 3]
        grads.append(own[...].astype(F32) + down[...].astype(F32) + up[...].astype(F32))
    grad = jnp.concatenate(
        [x[:, :QG] for x in grads]
        + [x[:, QG : QG + HEAD_DIM] for x in grads]
        + [x[:, QG + HEAD_DIM :] for x in grads],
        axis=1,
    )
    new[...], first_next[...], second_next[...] = mixed_step(
        w[...], grad, first[...], second[...], outer[...]
    )


def qkv_adam(idx, parts, w, first, second, outer):
    rows, width = w.shape
    block = 128
    steps = rows // block
    own = pl.BlockSpec((block, CG), lambda i, idx: (idx[0] * steps + i, 0))
    part = pl.BlockSpec((block, CG), lambda i, idx: (i, 0))
    full = pl.BlockSpec((block, width), lambda i, idx: (i, 0))
    return pl.pallas_call(
        qkv_adam_kernel,
        out_shape=(
            jax.ShapeDtypeStruct((rows, width), BF16),
            jax.ShapeDtypeStruct((rows, width), F32),
            jax.ShapeDtypeStruct((rows, width), F32),
        ),
        grid_spec=pltpu.PrefetchScalarGridSpec(
            num_scalar_prefetch=1,
            grid=(steps,),
            in_specs=[own, part, part] * KV_HEADS + [full] * 4,
            out_specs=(full, full, full),
        ),
        compiler_params=pltpu.CompilerParams(vmem_limit_bytes=VMEM_LIMIT),
        cost_estimate=pl.CostEstimate(flops=20_000_000, bytes_accessed=20_000_000, transcendentals=0),
    )(idx, *parts, w, first, second, outer)


def out_adam_kernel(parts_n, *refs):
    parts = refs[:parts_n]
    w, first, second, outer, new, first_next, second_next = refs[parts_n:]
    grad = parts[0][...].astype(F32)
    for part in parts[1:]:
        grad = grad + part[...].astype(F32)
    new[...], first_next[...], second_next[...] = mixed_step(
        w[...], grad, first[...], second[...], outer[...]
    )


def out_adam(parts, w, first, second, outer):
    rows, width = w.shape
    block = 64
    full = pl.BlockSpec((block, width), lambda i: (i, 0))
    return pl.pallas_call(
        functools.partial(out_adam_kernel, len(parts)),
        out_shape=(
            jax.ShapeDtypeStruct((rows, width), BF16),
            jax.ShapeDtypeStruct((rows, width), F32),
            jax.ShapeDtypeStruct((rows, width), F32),
        ),
        grid=(rows // block,),
        in_specs=[full] * (len(parts) + 4),
        out_specs=(full, full, full),
        compiler_params=pltpu.CompilerParams(vmem_limit_bytes=VMEM_LIMIT),
        cost_estimate=pl.CostEstimate(flops=20_000_000, bytes_accessed=14_000_000, transcendentals=0),
    )(*parts, w, first, second, outer)


def nesterov(global_value, momentum, average):
    delta = global_value - average
    momentum_next = OUTER_MOMENTUM * momentum + delta
    return (global_value - OUTER_RATE * (delta + OUTER_MOMENTUM * momentum_next), momentum_next)


def after(x, *others):
    return lax.optimization_barrier((x, *others))[0]


def line_gather(x, n, owners, first=None):
    got = {0: x}
    for way in (1, -1):
        held = x
        for s in range(1, n):
            pairs = [(i, i + way) for i in range(n) if 0 <= i + way < n and (i - way * (s - 1)) in owners]
            if not pairs:
                break
            held = lax.ppermute(held, "fsdp", pairs)
            got[way * s] = held
    return got


def line_reduce(blocks, n, owners, me):
    ends = []
    for way in (1, -1):
        held = None
        for s in range(1, n):
            if way < 0:
                dest = {i: s + i - n for i in range(n)}
            else:
                dest = {i: i + n - s for i in range(n)}
            pairs = [(i, i + way) for i in range(n) if 0 <= i + way < n and dest[i] in owners
                     and 0 <= dest[i] < n and (dest[i] - i) * way > 0]
            if not pairs:
                continue
            at = (me + (s - n) if way < 0 else me + (n - s)) - owners[0]
            block = lax.dynamic_index_in_dim(blocks, jnp.clip(at, 0, len(owners) - 1), 0, keepdims=False)
            if held is not None:
                block = (block.astype(F32) + held.astype(F32)).astype(BF16)
            held = lax.ppermute(block, "fsdp", pairs)
        ends.append(held)
    return ends


def all_sum(x, axis, n):
    k = 1
    while k < n:
        x = x + lax.ppermute(x, axis, [(i, i ^ k) for i in range(n)])
        k *= 2
    return x


def shards(
    tokens,
    cotangent,
    norm_gain,
    qkv_weight,
    out_weight,
    gain_first,
    gain_second,
    qkv_first,
    qkv_second,
    out_first,
    out_second,
    gain_global,
    gain_momentum,
    qkv_global,
    qkv_momentum,
    out_global,
    out_momentum,
):
    n = lax.axis_size("fsdp")
    islands = lax.axis_size("island")
    me = lax.axis_index("fsdp")
    idx = me[None].astype(jnp.int32)
    gain = norm_gain[0]
    w_qkv = qkv_weight[0]
    w_out = out_weight[0]
    rows, qkv_width = w_qkv.shape
    length, width = tokens.shape
    qw = HEADS * HEAD_DIM
    kw = KV_HEADS * HEAD_DIM
    per = n // KV_HEADS

    gathered = []
    previous = ()
    for g in ORDER:
        own = jnp.concatenate(
            [
                w_qkv[:, g * QG : (g + 1) * QG],
                w_qkv[:, qw + g * HEAD_DIM : qw + (g + 1) * HEAD_DIM],
                w_qkv[:, qw + kw + g * HEAD_DIM : qw + kw + (g + 1) * HEAD_DIM],
            ],
            axis=1,
        )
        out_own = w_out
        if previous:
            own, out_own = lax.optimization_barrier((own, out_own, *previous))[:2]
        owners = tuple(range(g * per, (g + 1) * per))
        q_cand = line_gather(own, n, tuple(range(n)))
        o_cand = line_gather(out_own, n, owners)
        previous = (q_cand[1], q_cand[-1])
        gathered.append((g, owners, q_cand, o_cand))

    wide = tokens.astype(F32)
    factor = lax.rsqrt(jnp.mean(wide * wide, axis=-1, keepdims=True) + NORM_EPS)
    normed = (wide * factor * gain).astype(BF16)
    normed_t = normed.T
    tab = rope_tables(length)

    gain_sum = jnp.zeros((8, width), F32)
    q_parts = [None] * KV_HEADS
    out_parts = []
    own_out = None
    for g, owners, q_cand, o_cand in gathered:
        g_qkv, g_out, gain_sum = group_step(
            n, owners, idx, normed, normed_t, cotangent, tab, gain_sum, q_cand, o_cand
        )
        up, down = line_reduce(g_qkv.reshape(n, rows, CG), n, tuple(range(n)), me)
        q_parts[g] = (g_qkv, down, up)
        blocks = g_out.reshape(per, g_out.shape[0] // per, width)
        ends = line_reduce(blocks, n, owners, me)
        out_parts += [x for x in ends if x is not None]
        mine = lax.dynamic_index_in_dim(blocks, jnp.clip(me - owners[0], 0, per - 1), 0, keepdims=False)
        here = jnp.logical_and(me >= owners[0], me <= owners[-1])
        own_out = mine if own_out is None else jnp.where(here, mine, own_out)

    gain_grad = all_sum(gain_sum[0], "fsdp", n) / gain
    gain_step, gain_first_next, gain_second_next = adam(gain, gain_grad, gain_first[0], gain_second[0], 0.0)

    scale = 1.0 / islands
    qkv_total = lax.psum_scatter(w_qkv, "island", scatter_dimension=1, tiled=True).astype(F32)
    out_total = lax.psum_scatter(w_out, "island", scatter_dimension=1, tiled=True).astype(F32)
    gain_total = all_sum(gain, "island", islands)
    gain_pair = nesterov(gain_global, gain_momentum, gain_total * scale)
    qkv_pair = nesterov(qkv_global, qkv_momentum, qkv_total * scale)
    out_pair = nesterov(out_global, out_momentum, out_total * scale)
    qkv_whole = lax.all_gather(qkv_pair[0].astype(BF16), "island", axis=1, tiled=True)
    out_whole = lax.all_gather(out_pair[0].astype(BF16), "island", axis=1, tiled=True)

    out_state = out_adam([own_out] + out_parts, w_out, out_first[0], out_second[0], out_whole)
    flat = [x for part in q_parts for x in part]
    qkv_state = qkv_adam(idx, flat, w_qkv, qkv_first[0], qkv_second[0], qkv_whole)
    gain_next = MIXING * gain_step + (1.0 - MIXING) * gain_pair[0]
    return (
        gain_next[None],
        qkv_state[0][None],
        out_state[0][None],
        gain_first_next[None],
        gain_second_next[None],
        qkv_state[1][None],
        qkv_state[2][None],
        out_state[1][None],
        out_state[2][None],
        gain_pair[0],
        gain_pair[1],
        qkv_pair[0],
        qkv_pair[1],
        out_pair[0],
        out_pair[1],
    )


def solution(mesh):
    placed = (
        P(("island", "fsdp"), None),
        P(("island", "fsdp"), None),
        P("island", None),
        P("island", "fsdp", None),
        P("island", "fsdp", None),
        P("island", None),
        P("island", None),
        P("island", "fsdp", None),
        P("island", "fsdp", None),
        P("island", "fsdp", None),
        P("island", "fsdp", None),
        P(),
        P(),
        P("fsdp", "island"),
        P("fsdp", "island"),
        P("fsdp", "island"),
        P("fsdp", "island"),
    )
    return jax.shard_map(
        shards,
        mesh=mesh,
        in_specs=placed,
        out_specs=(
            P("island", None),
            P("island", "fsdp", None),
            P("island", "fsdp", None),
            P("island", None),
            P("island", None),
            P("island", "fsdp", None),
            P("island", "fsdp", None),
            P("island", "fsdp", None),
            P("island", "fsdp", None),
            P(),
            P(),
            P("fsdp", "island"),
            P("fsdp", "island"),
            P("fsdp", "island"),
            P("fsdp", "island"),
        ),
        check_vma=False,
    )
```

```python
import functools

import jax
import jax.numpy as jnp
from jax import lax
from jax.experimental import pallas as pl
from jax.experimental.pallas import tpu as pltpu
from jax.sharding import PartitionSpec as P

HEADS = 16
KV_HEADS = 4
HEAD_DIM = 64
GROUP = HEADS // KV_HEADS
QP = 2 * GROUP * HEAD_DIM
CP = QP + 4 * HEAD_DIM

BETA_ONE = 0.9
BETA_TWO = 0.95
ADAM_EPS = 1e-08
INNER_RATE = 0.001
WEIGHT_DECAY = 0.1
STEP_COUNT = 100.0
OUTER_RATE = 0.7
OUTER_MOMENTUM = 0.9
MIXING = 0.5
NORM_EPS = 1e-05
ROPE_BASE = 500000.0
VMEM_LIMIT = 50 * 1024 * 1024

PAIRS = KV_HEADS // 2
F32 = jnp.float32
BF16 = jnp.bfloat16
NN = (((1,), (0,)), ((), ()))
NT = (((1,), (1,)), ((), ()))


def mm(a, b, dims=NN):
    return lax.dot_general(a, b, dims, preferred_element_type=F32)


def rope_tables(length):
    half = HEAD_DIM // 2
    freqs = ROPE_BASE ** (-jnp.arange(half, dtype=F32) / half)
    angles = jnp.arange(length, dtype=F32)[:, None] * freqs[None, :]
    cosine = jnp.cos(angles)
    sine = jnp.sin(angles)
    zero = jnp.zeros_like(sine)
    c = jnp.concatenate([cosine] * 4, axis=1)
    above = jnp.concatenate([zero, sine] * 2, axis=1)
    below = jnp.concatenate([-sine, zero] * 2, axis=1)
    return jnp.stack([c, above, below])


def turn(x, tab, sign):
    side = pltpu.roll(x, 32, 1) * tab[1] + pltpu.roll(x, 96, 1) * tab[2]
    return x * tab[0] + sign * side


def halves(x, at):
    lane = lax.broadcasted_iota(jnp.int32, x.shape, 1)
    alone = jnp.where((lane < HEAD_DIM) == (at == 0), x, 0.0)
    other = pltpu.roll(alone, HEAD_DIM, 1)
    pair = (alone, other) if at == 0 else (other, alone)
    return tuple(t.astype(BF16) for t in pair)


def added(total, part):
    return part if total is None else total + part


def forward_kernel(normed, w_q, w_k, w_v, cot, tab, q_ref, k_ref, v_ref, top_ref, low_ref, go_ref):
    length = normed.shape[0]
    step = length // 2
    x = normed[...]
    k_tile = turn(mm(x, w_k[...]), tab, 1.0).astype(BF16)
    v_tile = mm(x, w_v[...]).astype(BF16)
    k_ref[...] = k_tile
    v_ref[...] = v_tile
    row = lax.broadcasted_iota(jnp.int32, (step, step), 0)
    col = lax.broadcasted_iota(jnp.int32, (step, step), 1)
    causal = row >= col
    for group in range(2):
        keys = halves(k_tile.astype(F32), group)
        values = halves(v_tile.astype(F32), group)
        for pair in range(GROUP // 2):
            tile = group * (GROUP // 2) + pair
            cut = slice(tile * 128, tile * 128 + 128)
            q = turn(mm(x, w_q[:, cut]), tab, 1.0).astype(BF16).astype(F32) * HEAD_DIM**-0.5
            q = q.astype(BF16)
            q_ref[:, cut] = q
            att = [None] * 2
            for half in range(2):
                head = tile * 2 + half
                for blk in range(2):
                    r0 = blk * step
                    nk = r0 + step
                    s = mm(q[r0:nk], keys[half][:nk], NT)
                    last = jnp.where(causal, s[:, r0:], -1e30)
                    s = last if blk == 0 else jnp.concatenate([s[:, :r0], last], axis=1)
                    top = jnp.max(s, axis=1, keepdims=True)
                    e = jnp.exp(s - top)
                    p = (e * (1.0 / jnp.sum(e, axis=1, keepdims=True))).astype(BF16)
                    if blk == 0:
                        top_ref[head] = p
                    else:
                        low_ref[head] = p
                    att[blk] = added(att[blk], mm(p, values[half][:nk]))
            att = jnp.concatenate(att, axis=0).astype(BF16).astype(F32).T.astype(BF16)
            go_ref[cut, :] = mm(att, cot[...]).astype(BF16)


def backward_kernel(normed_t, w_q, w_k, w_v, cot, wo, tab, q_ref, k_ref, v_ref, top_ref, low_ref, gain_in, g_ref, gain_ref):
    length = cot.shape[0]
    step = length // 2
    dm = []
    dks = []
    dvs = []
    for group in range(2):
        keys = halves(k_ref[...].astype(F32), group)
        values = halves(v_ref[...].astype(F32), group)
        dk_t = [[None] * 2 for _ in range(2)]
        dv_t = [[None] * 2 for _ in range(2)]
        for pair in range(GROUP // 2):
            tile = group * (GROUP // 2) + pair
            cut = slice(tile * 128, tile * 128 + 128)
            da_f = mm(cot[...], wo[cut, :], NT)
            da = da_f.astype(BF16)
            da_t = da.astype(F32).T.astype(BF16)
            q_t = q_ref[:, cut].astype(F32).T.astype(BF16)
            dq = [None] * 2
            for half in range(2):
                head = tile * 2 + half
                key = keys[half]
                value = values[half]
                for blk in range(2):
                    r0 = blk * step
                    nk = r0 + step
                    pb = top_ref[head] if blk == 0 else low_ref[head]
                    p = pb.astype(F32)
                    dp = mm(da[r0:nk], value[:nk], NT)
                    ds = (p * (dp - jnp.sum(p * dp, axis=1, keepdims=True))).astype(BF16)
                    dq[blk] = added(dq[blk], mm(ds, key[:nk]))
                    dv = mm(da_t[:, r0:nk], pb)
                    dk = mm(q_t[:, r0:nk], ds)
                    for kb in range(blk + 1):
                        part = slice(kb * step, kb * step + step)
                        dv_t[half][kb] = added(dv_t[half][kb], dv[:, part])
                        dk_t[half][kb] = added(dk_t[half][kb], dk[:, part])
            dq = jnp.concatenate(dq, axis=0) * HEAD_DIM**-0.5
            dm.append(turn(dq, tab, -1.0).astype(BF16))
        dks.append([dk_t[0][kb][:HEAD_DIM] + dk_t[1][kb][HEAD_DIM:] for kb in range(2)])
        dvs.append([dv_t[0][kb][:HEAD_DIM] + dv_t[1][kb][HEAD_DIM:] for kb in range(2)])

    def joined(parts):
        return jnp.concatenate(
            [jnp.concatenate([parts[0][kb], parts[1][kb]], axis=0).T for kb in range(2)], axis=0
        )

    dm.append(turn(joined(dks), tab, -1.0).astype(BF16))
    dm.append(joined(dvs).astype(BF16))
    dm = jnp.concatenate(dm, axis=1)
    ones = jnp.ones((8, CP), BF16)
    block = 512
    for at in range(g_ref.shape[0] // block):
        cut = slice(at * block, at * block + block)
        g = mm(normed_t[cut, :], dm)
        g_ref[cut, :] = g.astype(BF16)
        w = jnp.concatenate([w_q[cut, :], w_k[cut, :], w_v[cut, :]], axis=1)
        prod = g * w.astype(F32)
        high = prod.astype(BF16)
        low = (prod - high.astype(F32)).astype(BF16)
        gain_ref[:, cut] = gain_in[:, cut] + mm(ones, high, NT) + mm(ones, low, NT)


def w_specs(width, pair=None):
    first_k = HEADS * HEAD_DIM // 128
    first_v = first_k + KV_HEADS * HEAD_DIM // 128

    def at(i):
        return i if pair is None else pair

    return [
        pl.BlockSpec((width, QP), lambda i: (0, at(i))),
        pl.BlockSpec((width, 128), lambda i: (0, first_k + at(i))),
        pl.BlockSpec((width, 128), lambda i: (0, first_v + at(i))),
    ]


def full_spec(x):
    return pl.BlockSpec(x.shape, lambda i: (0,) * len(x.shape))


def forward(normed, w, cot, tab):
    length, width = normed.shape
    step = length // 2
    outs = (
        jax.ShapeDtypeStruct((length, PAIRS * QP), BF16),
        jax.ShapeDtypeStruct((length, PAIRS * 128), BF16),
        jax.ShapeDtypeStruct((length, PAIRS * 128), BF16),
        jax.ShapeDtypeStruct((HEADS, step, step), BF16),
        jax.ShapeDtypeStruct((HEADS, step, length), BF16),
        jax.ShapeDtypeStruct((HEADS * HEAD_DIM, width), BF16),
    )
    return pl.pallas_call(
        forward_kernel,
        out_shape=outs,
        grid=(PAIRS,),
        in_specs=[full_spec(normed)] + w_specs(width) + [full_spec(cot), full_spec(tab)],
        out_specs=saved_specs(length) + (pl.BlockSpec((QP, width), lambda i: (i, 0)),),
        compiler_params=pltpu.CompilerParams(vmem_limit_bytes=VMEM_LIMIT),
        cost_estimate=pl.CostEstimate(flops=32_000_000_000, bytes_accessed=30_000_000, transcendentals=0),
    )(normed, w, w, w, cot, tab)


def saved_specs(length, pair=None):
    step = length // 2

    def at(i):
        return i if pair is None else pair

    return (
        pl.BlockSpec((length, QP), lambda i: (0, at(i))),
        pl.BlockSpec((length, 128), lambda i: (0, at(i))),
        pl.BlockSpec((length, 128), lambda i: (0, at(i))),
        pl.BlockSpec((2 * GROUP, step, step), lambda i: (at(i), 0, 0)),
        pl.BlockSpec((2 * GROUP, step, length), lambda i: (at(i), 0, 0)),
    )


def backward(pair, normed_t, w, cot, wo, tab, saved, gain_in):
    width = w.shape[0]
    outs = (
        jax.ShapeDtypeStruct((width, CP), BF16),
        jax.ShapeDtypeStruct((8, width), F32),
    )
    return pl.pallas_call(
        backward_kernel,
        out_shape=outs,
        grid=(1,),
        in_specs=[full_spec(normed_t)]
        + w_specs(width, pair)
        + [full_spec(cot), pl.BlockSpec((QP, width), lambda i: (pair, 0)), full_spec(tab)]
        + list(saved_specs(cot.shape[0], pair))
        + [full_spec(gain_in)],
        out_specs=tuple(full_spec(x) for x in outs),
        compiler_params=pltpu.CompilerParams(vmem_limit_bytes=VMEM_LIMIT),
        cost_estimate=pl.CostEstimate(flops=20_000_000_000, bytes_accessed=18_000_000, transcendentals=0),
    )(normed_t, w, w, w, cot, wo, tab, *saved, gain_in)


def adam(wide, grad, first, second, decay):
    first_next = BETA_ONE * first + (1.0 - BETA_ONE) * grad
    second_next = BETA_TWO * second + (1.0 - BETA_TWO) * grad * grad
    update = (
        first_next
        / (1.0 - BETA_ONE**STEP_COUNT)
        / (jnp.sqrt(second_next / (1.0 - BETA_TWO**STEP_COUNT)) + ADAM_EPS)
    )
    return (wide - INNER_RATE * (update + decay * wide), first_next, second_next)


def mixed_step(w, grad, first, second, outer):
    stepped, first_next, second_next = adam(w.astype(F32), grad, first, second, WEIGHT_DECAY)
    new = (MIXING * stepped + (1.0 - MIXING) * outer.astype(F32)).astype(BF16)
    return new, first_next, second_next


def adam_kernel(held, *refs):
    grad, w, first, second, outer = refs[:5]
    new, first_next, second_next = refs[5 + held :]
    new[...], first_next[...], second_next[...] = mixed_step(
        w[...], grad[...].astype(F32), first[...], second[...], outer[...]
    )


def qkv_adam(pair, grad, w, first, second, outer, held):
    rows, width = w.shape
    q_blocks = QP // 128
    first_k = HEADS * HEAD_DIM // 128
    first_v = first_k + KV_HEADS * HEAD_DIM // 128

    def column(j):
        return (0, jnp.where(j < q_blocks, pair * q_blocks + j, jnp.where(j == q_blocks, first_k, first_v) + pair))

    part = pl.BlockSpec((rows, 128), lambda j: (0, j))
    full = pl.BlockSpec((rows, 128), column)
    return pl.pallas_call(
        functools.partial(adam_kernel, len(held)),
        out_shape=(
            jax.ShapeDtypeStruct((rows, width), BF16),
            jax.ShapeDtypeStruct((rows, width), F32),
            jax.ShapeDtypeStruct((rows, width), F32),
        ),
        grid=(CP // 128,),
        in_specs=[part] + [full] * 4 + [pl.BlockSpec(memory_space=pl.ANY)] * len(held),
        out_specs=(full, full, full),
        input_output_aliases={5 + i: i for i in range(len(held))},
        compiler_params=pltpu.CompilerParams(vmem_limit_bytes=VMEM_LIMIT),
        cost_estimate=pl.CostEstimate(flops=20_000_000, bytes_accessed=10_000_000, transcendentals=0),
    )(grad, w, first, second, outer, *held)


def out_adam(grad, w, first, second, outer):
    rows, width = w.shape
    block = 64
    full = pl.BlockSpec((block, width), lambda i: (i, 0))
    return pl.pallas_call(
        functools.partial(adam_kernel, 0),
        out_shape=(
            jax.ShapeDtypeStruct((rows, width), BF16),
            jax.ShapeDtypeStruct((rows, width), F32),
            jax.ShapeDtypeStruct((rows, width), F32),
        ),
        grid=(rows // block,),
        in_specs=[full] * 5,
        out_specs=(full, full, full),
        compiler_params=pltpu.CompilerParams(vmem_limit_bytes=VMEM_LIMIT),
        cost_estimate=pl.CostEstimate(flops=20_000_000, bytes_accessed=14_000_000, transcendentals=0),
    )(grad, w, first, second, outer)


def nesterov(global_value, momentum, average):
    delta = global_value - average
    momentum_next = OUTER_MOMENTUM * momentum + delta
    return (global_value - OUTER_RATE * (delta + OUTER_MOMENTUM * momentum_next), momentum_next)


def after(x, *others):
    return lax.optimization_barrier((x, *others))[0]


def all_sum(x, axis, n):
    k = 1
    while k < n:
        x = x + lax.ppermute(x, axis, [(i, i ^ k) for i in range(n)])
        k *= 2
    return x


def shards(
    tokens,
    cotangent,
    norm_gain,
    qkv_weight,
    out_weight,
    gain_first,
    gain_second,
    qkv_first,
    qkv_second,
    out_first,
    out_second,
    gain_global,
    gain_momentum,
    qkv_global,
    qkv_momentum,
    out_global,
    out_momentum,
):
    n = lax.axis_size("fsdp")
    islands = lax.axis_size("island")
    gain = norm_gain[0]
    w_qkv = qkv_weight[0]
    w_out = out_weight[0]
    length, width = tokens.shape

    all_qkv = lax.all_gather(w_qkv, "fsdp", axis=0, tiled=True)

    wide = tokens.astype(F32)
    factor = lax.rsqrt(jnp.mean(wide * wide, axis=-1, keepdims=True) + NORM_EPS)
    normed = (wide * factor * gain).astype(BF16)
    normed_t = normed.T
    tab = rope_tables(length)
    all_out = lax.all_gather(after(w_out, all_qkv, normed, normed_t, tab), "fsdp", axis=0, tiled=True)

    *saved, g_out = forward(normed, all_qkv, cotangent, tab)
    out_grad = lax.psum_scatter(g_out, "fsdp", scatter_dimension=0, tiled=True)

    gain_sum = jnp.zeros((8, width), F32)
    qkv_grad = []
    for pair in range(PAIRS):
        grad, gain_sum = backward(
            pair, normed_t, all_qkv, cotangent, all_out, tab, saved, gain_sum
        )
        qkv_grad.append(lax.psum_scatter(grad, "fsdp", scatter_dimension=0, tiled=True))

    gain_grad = all_sum(gain_sum[0], "fsdp", n) / gain
    gain_step, gain_first_next, gain_second_next = adam(gain, gain_grad, gain_first[0], gain_second[0], 0.0)

    scale = 1.0 / islands
    qkv_total = lax.psum_scatter(w_qkv, "island", scatter_dimension=1, tiled=True).astype(F32)
    out_total = lax.psum_scatter(w_out, "island", scatter_dimension=1, tiled=True).astype(F32)
    gain_total = all_sum(gain, "island", islands)
    gain_pair = nesterov(gain_global, gain_momentum, gain_total * scale)
    qkv_pair = nesterov(qkv_global, qkv_momentum, qkv_total * scale)
    out_pair = nesterov(out_global, out_momentum, out_total * scale)
    qkv_whole = lax.all_gather(qkv_pair[0].astype(BF16), "island", axis=1, tiled=True)
    out_whole = lax.all_gather(out_pair[0].astype(BF16), "island", axis=1, tiled=True)

    out_state = out_adam(out_grad, w_out, out_first[0], out_second[0], out_whole)
    qkv_state = ()
    for pair in range(PAIRS):
        qkv_state = qkv_adam(
            pair, qkv_grad[pair], w_qkv, qkv_first[0], qkv_second[0], qkv_whole, qkv_state
        )
    gain_next = MIXING * gain_step + (1.0 - MIXING) * gain_pair[0]
    return (
        gain_next[None],
        qkv_state[0][None],
        out_state[0][None],
        gain_first_next[None],
        gain_second_next[None],
        qkv_state[1][None],
        qkv_state[2][None],
        out_state[1][None],
        out_state[2][None],
        gain_pair[0],
        gain_pair[1],
        qkv_pair[0],
        qkv_pair[1],
        out_pair[0],
        out_pair[1],
    )


def solution(mesh):
    placed = (
        P(("island", "fsdp"), None),
        P(("island", "fsdp"), None),
        P("island", None),
        P("island", "fsdp", None),
        P("island", "fsdp", None),
        P("island", None),
        P("island", None),
        P("island", "fsdp", None),
        P("island", "fsdp", None),
        P("island", "fsdp", None),
        P("island", "fsdp", None),
        P(),
        P(),
        P("fsdp", "island"),
        P("fsdp", "island"),
        P("fsdp", "island"),
        P("fsdp", "island"),
    )
    return jax.shard_map(
        shards,
        mesh=mesh,
        in_specs=placed,
        out_specs=(
            P("island", None),
            P("island", "fsdp", None),
            P("island", "fsdp", None),
            P("island", None),
            P("island", None),
            P("island", "fsdp", None),
            P("island", "fsdp", None),
            P("island", "fsdp", None),
            P("island", "fsdp", None),
            P(),
            P(),
            P("fsdp", "island"),
            P("fsdp", "island"),
            P("fsdp", "island"),
            P("fsdp", "island"),
        ),
        check_vma=False,
    )
```

```python
import functools

import jax
import jax.numpy as jnp
from jax import lax
from jax.experimental import pallas as pl
from jax.experimental.pallas import tpu as pltpu
from jax.sharding import PartitionSpec as P

HEADS = 16
KV_HEADS = 4
HEAD_DIM = 64
GROUP = HEADS // KV_HEADS
QP = 2 * GROUP * HEAD_DIM
CP = QP + 4 * HEAD_DIM

BETA_ONE = 0.9
BETA_TWO = 0.95
ADAM_EPS = 1e-08
INNER_RATE = 0.001
WEIGHT_DECAY = 0.1
STEP_COUNT = 100.0
OUTER_RATE = 0.7
OUTER_MOMENTUM = 0.9
MIXING = 0.5
NORM_EPS = 1e-05
ROPE_BASE = 500000.0
VMEM_LIMIT = 50 * 1024 * 1024

PAIRS = KV_HEADS // 2
F32 = jnp.float32
BF16 = jnp.bfloat16
NN = (((1,), (0,)), ((), ()))
NT = (((1,), (1,)), ((), ()))


def mm(a, b, dims=NN):
    return lax.dot_general(a, b, dims, preferred_element_type=F32)


def rope_tables(length):
    half = HEAD_DIM // 2
    freqs = ROPE_BASE ** (-jnp.arange(half, dtype=F32) / half)
    angles = jnp.arange(length, dtype=F32)[:, None] * freqs[None, :]
    cosine = jnp.cos(angles)
    sine = jnp.sin(angles)
    zero = jnp.zeros_like(sine)
    c = jnp.concatenate([cosine] * 4, axis=1)
    above = jnp.concatenate([zero, sine] * 2, axis=1)
    below = jnp.concatenate([-sine, zero] * 2, axis=1)
    return jnp.stack([c, above, below])


def turn(x, tab, sign):
    side = pltpu.roll(x, 32, 1) * tab[1] + pltpu.roll(x, 96, 1) * tab[2]
    return x * tab[0] + sign * side


def halves(x, at):
    lane = lax.broadcasted_iota(jnp.int32, x.shape, 1)
    alone = jnp.where((lane < HEAD_DIM) == (at == 0), x, 0.0)
    other = pltpu.roll(alone, HEAD_DIM, 1)
    pair = (alone, other) if at == 0 else (other, alone)
    return tuple(t.astype(BF16) for t in pair)


def added(total, part):
    return part if total is None else total + part


def forward_kernel(n_cand, starts, normed, cot, tab, *refs):
    cands = refs[:n_cand]
    q_ref, k_ref, v_ref, top_ref, low_ref, go_ref, w_ref, sems = refs[n_cand:]

    def copy_of(at):
        rows = cands[at].shape[0]
        to = pl.ds(pl.multiple_of(starts[at], rows), rows)
        return pltpu.make_async_copy(cands[at], w_ref.at[to], sems.at[at])

    for at in range(n_cand):
        @pl.when(starts[at] >= 0)
        def _(at=at):
            copy_of(at).start()
    for at in range(n_cand):
        @pl.when(starts[at] >= 0)
        def _(at=at):
            copy_of(at).wait()
    length = normed.shape[0]
    step = length // 2
    x = normed[...]
    k_tile = turn(mm(x, w_ref[:, QP : QP + 128]), tab, 1.0).astype(BF16)
    v_tile = mm(x, w_ref[:, QP + 128 :]).astype(BF16)
    k_ref[...] = k_tile
    v_ref[...] = v_tile
    row = lax.broadcasted_iota(jnp.int32, (step, step), 0)
    col = lax.broadcasted_iota(jnp.int32, (step, step), 1)
    causal = row >= col
    for group in range(2):
        keys = halves(k_tile.astype(F32), group)
        values = halves(v_tile.astype(F32), group)
        for pair in range(GROUP // 2):
            tile = group * (GROUP // 2) + pair
            cut = slice(tile * 128, tile * 128 + 128)
            q = turn(mm(x, w_ref[:, cut]), tab, 1.0).astype(BF16).astype(F32) * HEAD_DIM**-0.5
            q = q.astype(BF16)
            q_ref[:, cut] = q
            att = [None] * 2
            for half in range(2):
                head = tile * 2 + half
                for blk in range(2):
                    r0 = blk * step
                    nk = r0 + step
                    s = mm(q[r0:nk], keys[half][:nk], NT)
                    last = jnp.where(causal, s[:, r0:], -1e30)
                    s = last if blk == 0 else jnp.concatenate([s[:, :r0], last], axis=1)
                    top = jnp.max(s, axis=1, keepdims=True)
                    e = jnp.exp(s - top)
                    p = (e * (1.0 / jnp.sum(e, axis=1, keepdims=True))).astype(BF16)
                    if blk == 0:
                        top_ref[head] = p
                    else:
                        low_ref[head] = p
                    att[blk] = added(att[blk], mm(p, values[half][:nk]))
            att = jnp.concatenate(att, axis=0).astype(BF16).astype(F32).T.astype(BF16)
            go_ref[cut, :] = mm(att, cot[...]).astype(BF16)


def backward_kernel(normed_t, w_ref, cot, wo, tab, q_ref, k_ref, v_ref, top_ref, low_ref, gain_in, g_ref, gain_ref):
    length = cot.shape[0]
    step = length // 2
    dm = []
    dks = []
    dvs = []
    for group in range(2):
        keys = halves(k_ref[...].astype(F32), group)
        values = halves(v_ref[...].astype(F32), group)
        dk_t = [[None] * 2 for _ in range(2)]
        dv_t = [[None] * 2 for _ in range(2)]
        for pair in range(GROUP // 2):
            tile = group * (GROUP // 2) + pair
            cut = slice(tile * 128, tile * 128 + 128)
            da_f = mm(cot[...], wo[cut, :], NT)
            da = da_f.astype(BF16)
            da_t = da.astype(F32).T.astype(BF16)
            q_t = q_ref[:, cut].astype(F32).T.astype(BF16)
            dq = [None] * 2
            for half in range(2):
                head = tile * 2 + half
                key = keys[half]
                value = values[half]
                for blk in range(2):
                    r0 = blk * step
                    nk = r0 + step
                    pb = top_ref[head] if blk == 0 else low_ref[head]
                    p = pb.astype(F32)
                    dp = mm(da[r0:nk], value[:nk], NT)
                    ds = (p * (dp - jnp.sum(p * dp, axis=1, keepdims=True))).astype(BF16)
                    dq[blk] = added(dq[blk], mm(ds, key[:nk]))
                    dv = mm(da_t[:, r0:nk], pb)
                    dk = mm(q_t[:, r0:nk], ds)
                    for kb in range(blk + 1):
                        part = slice(kb * step, kb * step + step)
                        dv_t[half][kb] = added(dv_t[half][kb], dv[:, part])
                        dk_t[half][kb] = added(dk_t[half][kb], dk[:, part])
            dq = jnp.concatenate(dq, axis=0) * HEAD_DIM**-0.5
            dm.append(turn(dq, tab, -1.0).astype(BF16))
        dks.append([dk_t[0][kb][:HEAD_DIM] + dk_t[1][kb][HEAD_DIM:] for kb in range(2)])
        dvs.append([dv_t[0][kb][:HEAD_DIM] + dv_t[1][kb][HEAD_DIM:] for kb in range(2)])

    def joined(parts):
        return jnp.concatenate(
            [jnp.concatenate([parts[0][kb], parts[1][kb]], axis=0).T for kb in range(2)], axis=0
        )

    dm.append(turn(joined(dks), tab, -1.0).astype(BF16))
    dm.append(joined(dvs).astype(BF16))
    dm = jnp.concatenate(dm, axis=1)
    ones = jnp.ones((8, CP), BF16)
    block = 512
    for at in range(g_ref.shape[0] // block):
        cut = slice(at * block, at * block + block)
        g = mm(normed_t[cut, :], dm)
        g_ref[cut, :] = g.astype(BF16)
        prod = g * w_ref[cut, :].astype(F32)
        high = prod.astype(BF16)
        low = (prod - high.astype(F32)).astype(BF16)
        gain_ref[:, cut] = gain_in[:, cut] + mm(ones, high, NT) + mm(ones, low, NT)


def vmem_call(kernel, outs, n_hbm=0, hbm_at=0, smem=0, scratch=(), other=None):
    whole = pl.BlockSpec(memory_space=pltpu.VMEM)

    def call(*args):
        specs = [whole] * len(args)
        for i in range(smem):
            specs[i] = pl.BlockSpec(memory_space=pltpu.SMEM)
        for i in range(hbm_at, hbm_at + n_hbm):
            specs[i] = pl.BlockSpec(memory_space=pl.ANY)
        for i, spec in (other or {}).items():
            specs[i] = spec
        return pl.pallas_call(
            kernel,
            out_shape=outs,
            grid=(1,),
            in_specs=specs,
            out_specs=tuple(whole for _ in outs),
            scratch_shapes=list(scratch),
            compiler_params=pltpu.CompilerParams(vmem_limit_bytes=VMEM_LIMIT),
            cost_estimate=pl.CostEstimate(flops=1, bytes_accessed=1, transcendentals=0),
        )(*args)

    return call


def forward(starts, normed, cot, tab, cands):
    length, width = normed.shape
    step = length // 2
    heads = 2 * GROUP
    outs = (
        jax.ShapeDtypeStruct((length, QP), BF16),
        jax.ShapeDtypeStruct((length, 128), BF16),
        jax.ShapeDtypeStruct((length, 128), BF16),
        jax.ShapeDtypeStruct((heads, step, step), BF16),
        jax.ShapeDtypeStruct((heads, step, length), BF16),
        jax.ShapeDtypeStruct((QP, width), BF16),
        jax.ShapeDtypeStruct((width, CP), BF16),
    )
    call = vmem_call(
        functools.partial(forward_kernel, len(cands)),
        outs,
        n_hbm=len(cands),
        hbm_at=4,
        smem=1,
        scratch=[pltpu.SemaphoreType.DMA((len(cands),))],
    )
    return call(starts, normed, cot, tab, *cands)


def backward(pair, normed_t, w, cot, wo, tab, saved, gain_in):
    width = w.shape[0]
    rows = pl.BlockSpec((QP, width), lambda i: (pair, 0))
    outs = (
        jax.ShapeDtypeStruct((width, CP), BF16),
        jax.ShapeDtypeStruct((8, width), F32),
    )
    return vmem_call(backward_kernel, outs, other={3: rows})(normed_t, w, cot, wo, tab, *saved, gain_in)


def norm_kernel(x_ref, gain_ref, out_ref, out_t_ref):
    block = 128
    for at in range(x_ref.shape[0] // block):
        cut = slice(at * block, at * block + block)
        x = x_ref[cut, :].astype(F32)
        factor = lax.rsqrt(jnp.mean(x * x, axis=1, keepdims=True) + NORM_EPS)
        y = (x * factor * gain_ref[...]).astype(BF16)
        out_ref[cut, :] = y
        out_t_ref[:, cut] = y.astype(F32).T.astype(BF16)


def norm(tokens, gain):
    length, width = tokens.shape
    outs = (jax.ShapeDtypeStruct((length, width), BF16), jax.ShapeDtypeStruct((width, length), BF16))
    return vmem_call(norm_kernel, outs)(tokens, gain)


def adam(wide, grad, first, second, decay):
    first_next = BETA_ONE * first + (1.0 - BETA_ONE) * grad
    second_next = BETA_TWO * second + (1.0 - BETA_TWO) * grad * grad
    update = (
        first_next
        / (1.0 - BETA_ONE**STEP_COUNT)
        / (jnp.sqrt(second_next / (1.0 - BETA_TWO**STEP_COUNT)) + ADAM_EPS)
    )
    return (wide - INNER_RATE * (update + decay * wide), first_next, second_next)


def mixed_step(w, grad, first, second, outer):
    stepped, first_next, second_next = adam(w.astype(F32), grad, first, second, WEIGHT_DECAY)
    new = (MIXING * stepped + (1.0 - MIXING) * outer.astype(F32)).astype(BF16)
    return new, first_next, second_next


def adam_kernel(n_parts, held, idx_ref, *refs):
    grad = refs[0][0].astype(F32)
    for part in refs[1:n_parts]:
        grad = grad + part[0].astype(F32)
    w, first, second, outer = refs[n_parts : n_parts + 4]
    new, first_next, second_next = refs[n_parts + 4 + held :]
    new[...], first_next[...], second_next[...] = mixed_step(
        w[...], grad, first[...], second[...], outer[...]
    )


def adam_call(grid, block, part_at, full_at, idx, parts, w, first, second, outer, held):
    rows, width = w.shape

    def part_spec(at):
        return pl.BlockSpec((1,) + block, lambda j, idx: (idx[at],) + part_at(j))

    full = pl.BlockSpec(block, lambda j, idx: full_at(j))
    n_parts = len(parts)
    return pl.pallas_call(
        functools.partial(adam_kernel, n_parts, len(held)),
        out_shape=(
            jax.ShapeDtypeStruct((rows, width), BF16),
            jax.ShapeDtypeStruct((rows, width), F32),
            jax.ShapeDtypeStruct((rows, width), F32),
        ),
        grid_spec=pltpu.PrefetchScalarGridSpec(
            num_scalar_prefetch=1,
            grid=(grid,),
            in_specs=[part_spec(i) for i in range(n_parts)]
            + [full] * 4
            + [pl.BlockSpec(memory_space=pl.ANY)] * len(held),
            out_specs=(full, full, full),
        ),
        input_output_aliases={1 + n_parts + 4 + i: i for i in range(len(held))},
        compiler_params=pltpu.CompilerParams(vmem_limit_bytes=VMEM_LIMIT),
        cost_estimate=pl.CostEstimate(flops=20_000_000, bytes_accessed=14_000_000, transcendentals=0),
    )(idx, *parts, w, first, second, outer, *held)


def qkv_adam(pair, grad, w, first, second, outer, held):
    q_blocks = QP // 128
    first_k = HEADS * HEAD_DIM // 128
    first_v = first_k + KV_HEADS * HEAD_DIM // 128

    def column(j):
        return (0, jnp.where(j < q_blocks, pair * q_blocks + j, jnp.where(j == q_blocks, first_k, first_v) + pair))

    idx, parts = grad
    return adam_call(
        CP // 128, (w.shape[0], 128), lambda j: (0, j), column, idx, parts, w, first, second, outer, held
    )


def out_adam(grad, w, first, second, outer):
    rows, width = w.shape
    idx, parts = grad
    return adam_call(
        rows // 64, (64, width), lambda j: (j, 0), lambda j: (j, 0), idx, parts, w, first, second, outer, ()
    )


def nesterov(global_value, momentum, average):
    delta = global_value - average
    momentum_next = OUTER_MOMENTUM * momentum + delta
    return (global_value - OUTER_RATE * (delta + OUTER_MOMENTUM * momentum_next), momentum_next)


def after(x, *others):
    return lax.optimization_barrier((x, *others))[0]


def line_gather(x, me, before=None):
    middle = jnp.logical_or(me == 1, me == 2)
    near = jnp.where(me < 2, 2, 1)
    far = jnp.where(me < 2, 3, 0)
    pair = lax.ppermute(x, "fsdp", [(0, 1), (1, 0), (2, 3), (3, 2)])
    mid_near = lax.ppermute(x, "fsdp", [(1, 2), (2, 1)])
    waits = (pair, mid_near) if before is None else (pair, mid_near, before)
    pair, mid_near = lax.optimization_barrier(waits)[:2]
    mid_far = lax.ppermute(pair, "fsdp", [(1, 2), (2, 1)])
    end_near = lax.ppermute(mid_near, "fsdp", [(1, 0), (2, 3)])
    end_far = lax.ppermute(mid_far, "fsdp", [(1, 0), (2, 3)])
    blocks = (x, pair, mid_near, mid_far, end_near, end_far)
    places = (
        me,
        me ^ 1,
        jnp.where(middle, near, -1),
        jnp.where(middle, far, -1),
        jnp.where(middle, -1, near),
        jnp.where(middle, -1, far),
    )
    return blocks, places


def gather(x, n, me, before=None):
    if n == 4:
        blocks, places = line_gather(x, me, before)
    else:
        blocks, places = (lax.all_gather(x, "fsdp", axis=0, tiled=True),), (me * 0,)
    starts = jnp.stack([p * x.shape[0] for p in places]).astype(jnp.int32)
    return blocks, starts


def scatter(x, n, me):
    rows = x.shape[0] // n
    blocks = x.reshape(n, rows, x.shape[1])
    if n != 4:
        return jnp.zeros((1,), jnp.int32), (lax.psum_scatter(x, "fsdp", scatter_dimension=0, tiled=True)[None],)

    def two(at):
        return lax.dynamic_slice_in_dim(blocks, at, 2, 0)

    def plus(a, b):
        return (a.astype(F32) + b.astype(F32)).astype(BF16)

    inward = lax.ppermute(two(jnp.where(me == 0, 2, 0)), "fsdp", [(3, 2), (0, 1)])
    across = lax.ppermute(plus(two(jnp.where(me == 1, 2, 0)), inward), "fsdp", [(2, 1), (1, 2)])
    passed = lax.dynamic_index_in_dim(across, jnp.where(me == 1, 0, 1), 0, keepdims=True)
    other = lax.dynamic_index_in_dim(blocks, me ^ 1, 0, keepdims=True)
    outward = lax.ppermute(plus(other, passed), "fsdp", [(0, 1), (1, 0), (2, 3), (3, 2)])
    idx = jnp.stack([me, jnp.where(me == 1, 1, 0), me * 0]).astype(jnp.int32)
    return idx, (blocks, across, outward)


def all_sum(x, axis, n):
    k = 1
    while k < n:
        x = x + lax.ppermute(x, axis, [(i, i ^ k) for i in range(n)])
        k *= 2
    return x


def shards(
    tokens,
    cotangent,
    norm_gain,
    qkv_weight,
    out_weight,
    gain_first,
    gain_second,
    qkv_first,
    qkv_second,
    out_first,
    out_second,
    gain_global,
    gain_momentum,
    qkv_global,
    qkv_momentum,
    out_global,
    out_momentum,
):
    n = lax.axis_size("fsdp")
    islands = lax.axis_size("island")
    gain = norm_gain[0]
    w_qkv = qkv_weight[0]
    w_out = out_weight[0]
    length, width = tokens.shape

    me = lax.axis_index("fsdp")
    qw = HEADS * HEAD_DIM
    kw = KV_HEADS * HEAD_DIM

    got = []
    for pair in range(PAIRS):
        own = jnp.concatenate(
            [
                w_qkv[:, pair * QP : (pair + 1) * QP],
                w_qkv[:, qw + pair * 128 : qw + (pair + 1) * 128],
                w_qkv[:, qw + kw + pair * 128 : qw + kw + (pair + 1) * 128],
            ],
            axis=1,
        )
        if got:
            own = after(own, *got[0][0][3:5])
        got.append(gather(own, n, me, got[0][0][-1] if got else None))
    all_out = lax.all_gather(after(w_out, *got[0][0][3:5]), "fsdp", axis=0, tiled=True)

    normed, normed_t = norm(tokens, gain[None])
    tab = rope_tables(length)

    scale = 1.0 / islands
    qkv_total = lax.psum_scatter(w_qkv, "island", scatter_dimension=1, tiled=True).astype(F32)
    out_total = lax.psum_scatter(w_out, "island", scatter_dimension=1, tiled=True).astype(F32)
    gain_total = all_sum(gain, "island", islands)
    gain_pair = nesterov(gain_global, gain_momentum, gain_total * scale)
    qkv_pair = nesterov(qkv_global, qkv_momentum, qkv_total * scale)
    out_pair = nesterov(out_global, out_momentum, out_total * scale)
    saved = []
    g_out = []
    for pair in range(PAIRS):
        blocks, starts = got[pair]
        if pair:
            starts = after(starts, qkv_pair[0], qkv_pair[1], out_pair[0], out_pair[1])
        *kept, grad, w_pair = forward(starts, normed, cotangent, tab, blocks)
        saved.append((kept, w_pair))
        g_out.append(grad)
    out_grad = scatter(jnp.concatenate(g_out, axis=0), n, me)

    gain_sum = after(jnp.zeros((8, width), F32), *g_out)
    qkv_grad = []
    for pair in range(PAIRS):
        kept, w_pair = saved[pair]
        grad, gain_sum = backward(pair, normed_t, w_pair, cotangent, all_out, tab, kept, gain_sum)
        qkv_grad.append(scatter(grad, n, me))

    gain_grad = all_sum(gain_sum[0], "fsdp", n) / gain
    gain_step, gain_first_next, gain_second_next = adam(gain, gain_grad, gain_first[0], gain_second[0], 0.0)

    qkv_whole = lax.all_gather(after(qkv_pair[0].astype(BF16), g_out[1]), "island", axis=1, tiled=True)
    out_whole = lax.all_gather(after(out_pair[0].astype(BF16), g_out[1]), "island", axis=1, tiled=True)

    out_state = out_adam(out_grad, w_out, out_first[0], out_second[0], out_whole)
    qkv_state = ()
    for pair in range(PAIRS):
        qkv_state = qkv_adam(
            pair, qkv_grad[pair], w_qkv, qkv_first[0], qkv_second[0], qkv_whole, qkv_state
        )
    gain_next = MIXING * gain_step + (1.0 - MIXING) * gain_pair[0]
    return (
        gain_next[None],
        qkv_state[0][None],
        out_state[0][None],
        gain_first_next[None],
        gain_second_next[None],
        qkv_state[1][None],
        qkv_state[2][None],
        out_state[1][None],
        out_state[2][None],
        gain_pair[0],
        gain_pair[1],
        qkv_pair[0],
        qkv_pair[1],
        out_pair[0],
        out_pair[1],
    )


def solution(mesh):
    placed = (
        P(("island", "fsdp"), None),
        P(("island", "fsdp"), None),
        P("island", None),
        P("island", "fsdp", None),
        P("island", "fsdp", None),
        P("island", None),
        P("island", None),
        P("island", "fsdp", None),
        P("island", "fsdp", None),
        P("island", "fsdp", None),
        P("island", "fsdp", None),
        P(),
        P(),
        P("fsdp", "island"),
        P("fsdp", "island"),
        P("fsdp", "island"),
        P("fsdp", "island"),
    )
    return jax.shard_map(
        shards,
        mesh=mesh,
        in_specs=placed,
        out_specs=(
            P("island", None),
            P("island", "fsdp", None),
            P("island", "fsdp", None),
            P("island", None),
            P("island", None),
            P("island", "fsdp", None),
            P("island", "fsdp", None),
            P("island", "fsdp", None),
            P("island", "fsdp", None),
            P(),
            P(),
            P("fsdp", "island"),
            P("fsdp", "island"),
            P("fsdp", "island"),
            P("fsdp", "island"),
        ),
        check_vma=False,
    )
```

```python
import functools

import jax
import jax.numpy as jnp
from jax import lax
from jax.experimental import pallas as pl
from jax.experimental.pallas import tpu as pltpu
from jax.sharding import PartitionSpec as P

HEADS = 16
KV_HEADS = 4
HEAD_DIM = 64
GROUP = HEADS // KV_HEADS
QP = 2 * GROUP * HEAD_DIM
CP = QP + 4 * HEAD_DIM

BETA_ONE = 0.9
BETA_TWO = 0.95
ADAM_EPS = 1e-08
INNER_RATE = 0.001
WEIGHT_DECAY = 0.1
STEP_COUNT = 100.0
OUTER_RATE = 0.7
OUTER_MOMENTUM = 0.9
MIXING = 0.5
NORM_EPS = 1e-05
ROPE_BASE = 500000.0
VMEM_LIMIT = 50 * 1024 * 1024

PAIRS = KV_HEADS // 2
F32 = jnp.float32
BF16 = jnp.bfloat16
NN = (((1,), (0,)), ((), ()))
NT = (((1,), (1,)), ((), ()))


def mm(a, b, dims=NN):
    return lax.dot_general(a, b, dims, preferred_element_type=F32)


def rope_tables(length):
    half = HEAD_DIM // 2
    freqs = ROPE_BASE ** (-jnp.arange(half, dtype=F32) / half)
    angles = jnp.arange(length, dtype=F32)[:, None] * freqs[None, :]
    cosine = jnp.cos(angles)
    sine = jnp.sin(angles)
    zero = jnp.zeros_like(sine)
    c = jnp.concatenate([cosine] * 4, axis=1)
    above = jnp.concatenate([zero, sine] * 2, axis=1)
    below = jnp.concatenate([-sine, zero] * 2, axis=1)
    return jnp.stack([c, above, below])


def turn(x, tab, sign):
    side = pltpu.roll(x, 32, 1) * tab[1] + pltpu.roll(x, 96, 1) * tab[2]
    return x * tab[0] + sign * side


def halves(x, at):
    lane = lax.broadcasted_iota(jnp.int32, x.shape, 1)
    alone = jnp.where((lane < HEAD_DIM) == (at == 0), x, 0.0)
    other = pltpu.roll(alone, HEAD_DIM, 1)
    pair = (alone, other) if at == 0 else (other, alone)
    return tuple(t.astype(BF16) for t in pair)


def added(total, part):
    return part if total is None else total + part


def assemble(starts, cands, whole, sems):
    def copy_of(at):
        rows = cands[at].shape[0]
        to = pl.ds(pl.multiple_of(starts[at], rows), rows)
        return pltpu.make_async_copy(cands[at], whole.at[to], sems.at[at])

    for at in range(len(cands)):
        @pl.when(starts[at] >= 0)
        def _(at=at):
            copy_of(at).start()
    for at in range(len(cands)):
        @pl.when(starts[at] >= 0)
        def _(at=at):
            copy_of(at).wait()


def forward_kernel(n_cand, starts, normed, cot, tab, *refs):
    cands = refs[:n_cand]
    q_ref, k_ref, v_ref, top_ref, low_ref, go_ref, w_ref, sems = refs[n_cand:]

    assemble(starts, cands, w_ref, sems)
    length = normed.shape[0]
    step = length // 2
    x = normed[...]
    k_tile = turn(mm(x, w_ref[:, QP : QP + 128]), tab, 1.0).astype(BF16)
    v_tile = mm(x, w_ref[:, QP + 128 :]).astype(BF16)
    k_ref[...] = k_tile
    v_ref[...] = v_tile
    row = lax.broadcasted_iota(jnp.int32, (step, step), 0)
    col = lax.broadcasted_iota(jnp.int32, (step, step), 1)
    causal = row >= col
    for group in range(2):
        keys = halves(k_tile.astype(F32), group)
        values = halves(v_tile.astype(F32), group)
        for pair in range(GROUP // 2):
            tile = group * (GROUP // 2) + pair
            cut = slice(tile * 128, tile * 128 + 128)
            q = turn(mm(x, w_ref[:, cut]), tab, 1.0).astype(BF16).astype(F32) * HEAD_DIM**-0.5
            q = q.astype(BF16)
            q_ref[:, cut] = q
            att = [None] * 2
            for half in range(2):
                head = tile * 2 + half
                for blk in range(2):
                    r0 = blk * step
                    nk = r0 + step
                    s = mm(q[r0:nk], keys[half][:nk], NT)
                    last = jnp.where(causal, s[:, r0:], -1e30)
                    s = last if blk == 0 else jnp.concatenate([s[:, :r0], last], axis=1)
                    top = jnp.max(s, axis=1, keepdims=True)
                    e = jnp.exp(s - top)
                    p = (e * (1.0 / jnp.sum(e, axis=1, keepdims=True))).astype(BF16)
                    if blk == 0:
                        top_ref[head] = p
                    else:
                        low_ref[head] = p
                    att[blk] = added(att[blk], mm(p, values[half][:nk]))
            att = jnp.concatenate(att, axis=0).astype(BF16).astype(F32).T.astype(BF16)
            go_ref[cut, :] = mm(att, cot[...]).astype(BF16)


def backward_kernel(n_cand, starts, normed_t, w_ref, cot, tab, q_ref, k_ref, v_ref, top_ref, low_ref, gain_in, *refs):
    cands = refs[:n_cand]
    g_ref, gain_ref, wo, sems = refs[n_cand:]
    assemble(starts, cands, wo, sems)
    length = cot.shape[0]
    step = length // 2
    dm = []
    dks = []
    dvs = []
    for group in range(2):
        keys = halves(k_ref[...].astype(F32), group)
        values = halves(v_ref[...].astype(F32), group)
        dk_t = [[None] * 2 for _ in range(2)]
        dv_t = [[None] * 2 for _ in range(2)]
        for pair in range(GROUP // 2):
            tile = group * (GROUP // 2) + pair
            cut = slice(tile * 128, tile * 128 + 128)
            da_f = mm(cot[...], wo[cut, :], NT)
            da = da_f.astype(BF16)
            da_t = da.astype(F32).T.astype(BF16)
            q_t = q_ref[:, cut].astype(F32).T.astype(BF16)
            dq = [None] * 2
            for half in range(2):
                head = tile * 2 + half
                key = keys[half]
                value = values[half]
                for blk in range(2):
                    r0 = blk * step
                    nk = r0 + step
                    pb = top_ref[head] if blk == 0 else low_ref[head]
                    p = pb.astype(F32)
                    dp = mm(da[r0:nk], value[:nk], NT)
                    ds = (p * (dp - jnp.sum(p * dp, axis=1, keepdims=True))).astype(BF16)
                    dq[blk] = added(dq[blk], mm(ds, key[:nk]))
                    dv = mm(da_t[:, r0:nk], pb)
                    dk = mm(q_t[:, r0:nk], ds)
                    for kb in range(blk + 1):
                        part = slice(kb * step, kb * step + step)
                        dv_t[half][kb] = added(dv_t[half][kb], dv[:, part])
                        dk_t[half][kb] = added(dk_t[half][kb], dk[:, part])
            dq = jnp.concatenate(dq, axis=0) * HEAD_DIM**-0.5
            dm.append(turn(dq, tab, -1.0).astype(BF16))
        dks.append([dk_t[0][kb][:HEAD_DIM] + dk_t[1][kb][HEAD_DIM:] for kb in range(2)])
        dvs.append([dv_t[0][kb][:HEAD_DIM] + dv_t[1][kb][HEAD_DIM:] for kb in range(2)])

    def joined(parts):
        return jnp.concatenate(
            [jnp.concatenate([parts[0][kb], parts[1][kb]], axis=0).T for kb in range(2)], axis=0
        )

    dm.append(turn(joined(dks), tab, -1.0).astype(BF16))
    dm.append(joined(dvs).astype(BF16))
    dm = jnp.concatenate(dm, axis=1)
    ones = jnp.ones((8, CP), BF16)
    block = 512
    for at in range(g_ref.shape[0] // block):
        cut = slice(at * block, at * block + block)
        g = mm(normed_t[cut, :], dm)
        g_ref[cut, :] = g.astype(BF16)
        prod = g * w_ref[cut, :].astype(F32)
        high = prod.astype(BF16)
        low = (prod - high.astype(F32)).astype(BF16)
        gain_ref[:, cut] = gain_in[:, cut] + mm(ones, high, NT) + mm(ones, low, NT)


def vmem_call(kernel, outs, n_hbm=0, hbm_at=0, smem=0, scratch=()):
    whole = pl.BlockSpec(memory_space=pltpu.VMEM)

    def call(*args):
        specs = [whole] * len(args)
        for i in range(smem):
            specs[i] = pl.BlockSpec(memory_space=pltpu.SMEM)
        for i in range(hbm_at, hbm_at + n_hbm):
            specs[i] = pl.BlockSpec(memory_space=pl.ANY)
        return pl.pallas_call(
            kernel,
            out_shape=outs,
            grid=(1,),
            in_specs=specs,
            out_specs=tuple(whole for _ in outs),
            scratch_shapes=list(scratch),
            compiler_params=pltpu.CompilerParams(vmem_limit_bytes=VMEM_LIMIT),
            cost_estimate=pl.CostEstimate(flops=1, bytes_accessed=1, transcendentals=0),
        )(*args)

    return call


def forward(starts, normed, cot, tab, cands):
    length, width = normed.shape
    step = length // 2
    heads = 2 * GROUP
    outs = (
        jax.ShapeDtypeStruct((length, QP), BF16),
        jax.ShapeDtypeStruct((length, 128), BF16),
        jax.ShapeDtypeStruct((length, 128), BF16),
        jax.ShapeDtypeStruct((heads, step, step), BF16),
        jax.ShapeDtypeStruct((heads, step, length), BF16),
        jax.ShapeDtypeStruct((QP, width), BF16),
        jax.ShapeDtypeStruct((width, CP), BF16),
    )
    call = vmem_call(
        functools.partial(forward_kernel, len(cands)),
        outs,
        n_hbm=len(cands),
        hbm_at=4,
        smem=1,
        scratch=[pltpu.SemaphoreType.DMA((len(cands),))],
    )
    return call(starts, normed, cot, tab, *cands)


def backward(starts, normed_t, w, cot, tab, saved, gain_in, cands):
    width = w.shape[0]
    outs = (
        jax.ShapeDtypeStruct((width, CP), BF16),
        jax.ShapeDtypeStruct((8, width), F32),
    )
    call = vmem_call(
        functools.partial(backward_kernel, len(cands)),
        outs,
        n_hbm=len(cands),
        hbm_at=6 + len(saved),
        smem=1,
        scratch=[pltpu.VMEM((QP, width), BF16), pltpu.SemaphoreType.DMA((len(cands),))],
    )
    return call(starts, normed_t, w, cot, tab, *saved, gain_in, *cands)


def norm_kernel(x_ref, gain_ref, out_ref, out_t_ref):
    block = 128
    for at in range(x_ref.shape[0] // block):
        cut = slice(at * block, at * block + block)
        x = x_ref[cut, :].astype(F32)
        factor = lax.rsqrt(jnp.mean(x * x, axis=1, keepdims=True) + NORM_EPS)
        y = (x * factor * gain_ref[...]).astype(BF16)
        out_ref[cut, :] = y
        out_t_ref[:, cut] = y.astype(F32).T.astype(BF16)


def norm(tokens, gain):
    length, width = tokens.shape
    outs = (jax.ShapeDtypeStruct((length, width), BF16), jax.ShapeDtypeStruct((width, length), BF16))
    return vmem_call(norm_kernel, outs)(tokens, gain)


def adam(wide, grad, first, second, decay):
    first_next = BETA_ONE * first + (1.0 - BETA_ONE) * grad
    second_next = BETA_TWO * second + (1.0 - BETA_TWO) * grad * grad
    update = (
        first_next
        / (1.0 - BETA_ONE**STEP_COUNT)
        / (jnp.sqrt(second_next / (1.0 - BETA_TWO**STEP_COUNT)) + ADAM_EPS)
    )
    return (wide - INNER_RATE * (update + decay * wide), first_next, second_next)


def mixed_step(w, grad, first, second, outer):
    stepped, first_next, second_next = adam(w.astype(F32), grad, first, second, WEIGHT_DECAY)
    new = (MIXING * stepped + (1.0 - MIXING) * outer.astype(F32)).astype(BF16)
    return new, first_next, second_next


def adam_kernel(n_parts, held, idx_ref, *refs):
    grad = refs[0][0].astype(F32)
    for part in refs[1:n_parts]:
        grad = grad + part[0].astype(F32)
    w, first, second, outer = refs[n_parts : n_parts + 4]
    new, first_next, second_next = refs[n_parts + 4 + held :]
    new[...], first_next[...], second_next[...] = mixed_step(
        w[...], grad, first[...], second[...], outer[...]
    )


def adam_call(grid, block, part_at, full_at, idx, parts, w, first, second, outer, held):
    rows, width = w.shape

    def part_spec(at):
        return pl.BlockSpec((1,) + block, lambda j, idx: (idx[at],) + part_at(j))

    full = pl.BlockSpec(block, lambda j, idx: full_at(j))
    n_parts = len(parts)
    return pl.pallas_call(
        functools.partial(adam_kernel, n_parts, len(held)),
        out_shape=(
            jax.ShapeDtypeStruct((rows, width), BF16),
            jax.ShapeDtypeStruct((rows, width), F32),
            jax.ShapeDtypeStruct((rows, width), F32),
        ),
        grid_spec=pltpu.PrefetchScalarGridSpec(
            num_scalar_prefetch=1,
            grid=(grid,),
            in_specs=[part_spec(i) for i in range(n_parts)]
            + [full] * 4
            + [pl.BlockSpec(memory_space=pl.ANY)] * len(held),
            out_specs=(full, full, full),
        ),
        input_output_aliases={1 + n_parts + 4 + i: i for i in range(len(held))},
        compiler_params=pltpu.CompilerParams(vmem_limit_bytes=VMEM_LIMIT),
        cost_estimate=pl.CostEstimate(flops=20_000_000, bytes_accessed=14_000_000, transcendentals=0),
    )(idx, *parts, w, first, second, outer, *held)


def qkv_adam(pair, grad, w, first, second, outer, held):
    q_blocks = QP // 128
    first_k = HEADS * HEAD_DIM // 128
    first_v = first_k + KV_HEADS * HEAD_DIM // 128

    def column(j):
        return (0, jnp.where(j < q_blocks, pair * q_blocks + j, jnp.where(j == q_blocks, first_k, first_v) + pair))

    idx, parts = grad
    return adam_call(
        CP // 128, (w.shape[0], 128), lambda j: (0, j), column, idx, parts, w, first, second, outer, held
    )


def out_adam(grad, w, first, second, outer):
    rows, width = w.shape
    idx, parts = grad
    return adam_call(
        rows // 64, (64, width), lambda j: (j, 0), lambda j: (j, 0), idx, parts, w, first, second, outer, ()
    )


def nesterov(global_value, momentum, average):
    delta = global_value - average
    momentum_next = OUTER_MOMENTUM * momentum + delta
    return (global_value - OUTER_RATE * (delta + OUTER_MOMENTUM * momentum_next), momentum_next)


def after(x, *others):
    return lax.optimization_barrier((x, *others))[0]


PAIR_SWAP = [(0, 1), (1, 0), (2, 3), (3, 2)]
MID_SWAP = [(1, 2), (2, 1)]
INWARD = [(0, 1), (3, 2)]
OUTWARD = [(1, 0), (2, 3)]


def send(x, pairs):
    return lax.ppermute(x, "fsdp", pairs)


def table(me, *values):
    return jnp.array(values, jnp.int32)[me]


def plus(a, b):
    return (a.astype(F32) + b.astype(F32)).astype(BF16)


def block(x, at):
    return lax.dynamic_slice_in_dim(x, at, 1, 0)


def starts_of(rows, places):
    return jnp.stack([jnp.where(p < 0, -1, p * rows) for p in places]).astype(jnp.int32)


def line_starts(me, rows):
    return starts_of(
        rows,
        (
            me,
            me ^ 1,
            table(me, -1, 2, 1, -1),
            table(me, -1, 3, 0, -1),
            table(me, 2, -1, -1, 1),
            table(me, 3, -1, -1, 0),
        ),
    )


def scatter_merged(x, me):
    blocks = x.reshape(4, x.shape[0] // 4, x.shape[1])

    def two(at):
        return lax.dynamic_slice_in_dim(blocks, at, 2, 0)

    inward = send(two(table(me, 2, 0, 0, 0)), INWARD)
    across = send(plus(two(table(me, 0, 2, 0, 0)), inward), MID_SWAP)
    outward = send(plus(block(blocks, me ^ 1), block(across, table(me, 0, 0, 1, 0))), PAIR_SWAP)
    idx = jnp.stack([me, table(me, 0, 1, 0, 0), me * 0]).astype(jnp.int32)
    return idx, (blocks, across, outward)


def scatter_single(x, me, before):
    blocks = x.reshape(4, x.shape[0] // 4, x.shape[1])
    far_in = send(block(blocks, 3 - me), INWARD)
    near_in = send(block(blocks, table(me, 2, 0, 0, 1)), INWARD)
    far = send(plus(block(blocks, table(me, 0, 3, 0, 0)), far_in), MID_SWAP)
    near = send(plus(block(blocks, 3 - me), near_in), MID_SWAP)
    outward = send(after(plus(block(blocks, me ^ 1), far), *before), PAIR_SWAP)
    idx = jnp.stack([me, me * 0, me * 0]).astype(jnp.int32)
    return idx, (blocks, near, outward)


def all_sum(x, axis, n):
    k = 1
    while k < n:
        x = x + lax.ppermute(x, axis, [(i, i ^ k) for i in range(n)])
        k *= 2
    return x


def shards(
    tokens,
    cotangent,
    norm_gain,
    qkv_weight,
    out_weight,
    gain_first,
    gain_second,
    qkv_first,
    qkv_second,
    out_first,
    out_second,
    gain_global,
    gain_momentum,
    qkv_global,
    qkv_momentum,
    out_global,
    out_momentum,
):
    n = lax.axis_size("fsdp")
    islands = lax.axis_size("island")
    gain = norm_gain[0]
    w_qkv = qkv_weight[0]
    w_out = out_weight[0]
    length, width = tokens.shape

    me = lax.axis_index("fsdp")
    qw = HEADS * HEAD_DIM
    kw = KV_HEADS * HEAD_DIM

    packed = [
        jnp.concatenate(
            [
                w_qkv[:, pair * QP : (pair + 1) * QP],
                w_qkv[:, qw + pair * 128 : qw + (pair + 1) * 128],
                w_qkv[:, qw + kw + pair * 128 : qw + kw + (pair + 1) * 128],
            ],
            axis=1,
        )
        for pair in range(PAIRS)
    ]
    w_rows = w_qkv.shape[0]
    o_rows = w_out.shape[0]
    line = n == 4

    if line:
        x0, x1 = packed
        pair0 = send(x0, PAIR_SWAP)
        near0 = send(x0, MID_SWAP)
        normed, normed_t = norm(tokens, gain[None])
        tab = rope_tables(length)
        pair0, near0, normed, normed_t, tab = lax.optimization_barrier((pair0, near0, normed, normed_t, tab))
        far0 = send(pair0, MID_SWAP)
        end_near0 = send(near0, OUTWARD)
        o_in = send(after(w_out, pair0, near0), INWARD)
        far0, end_near0 = lax.optimization_barrier((far0, end_near0))
        end_far0 = send(far0, OUTWARD)
        o_near = send(after(w_out, far0), MID_SWAP)
        o_far = send(after(o_in, far0), MID_SWAP)
        o_one = send(jnp.where(me == 1, w_out, o_near), OUTWARD)
        q_cands = [(x0, pair0, near0, far0, end_near0, end_far0)]
        q_starts = line_starts(me, w_rows)
    else:
        normed, normed_t = norm(tokens, gain[None])
        tab = rope_tables(length)
        q_cands = [(lax.all_gather(x, "fsdp", axis=0, tiled=True),) for x in packed]
        q_starts = starts_of(0, (me,))
        all_out = lax.all_gather(w_out, "fsdp", axis=0, tiled=True)

    scale = 1.0 / islands
    qkv_total = lax.psum_scatter(w_qkv, "island", scatter_dimension=1, tiled=True).astype(F32)
    out_total = lax.psum_scatter(w_out, "island", scatter_dimension=1, tiled=True).astype(F32)
    gain_total = all_sum(gain, "island", islands)
    gain_pair = nesterov(gain_global, gain_momentum, gain_total * scale)
    qkv_pair = nesterov(qkv_global, qkv_momentum, qkv_total * scale)
    out_pair = nesterov(out_global, out_momentum, out_total * scale)
    qkv_whole = lax.all_gather(qkv_pair[0].astype(BF16), "island", axis=1, tiled=True)
    out_whole = lax.all_gather(out_pair[0].astype(BF16), "island", axis=1, tiled=True)

    *kept0, go0, w0 = forward(q_starts, normed, cotangent, tab, q_cands[0])
    gain_sum = jnp.zeros((8, width), F32)
    if line:
        go0 = go0.reshape(2, o_rows, width)
        o_two = send(after(o_far, go0), OUTWARD)
        go_in0 = send(go0, [(3, 2)])
        synced = (qkv_pair[0], qkv_pair[1], out_pair[0], out_pair[1])
        x1 = after(x1, o_two)
        pair1 = send(x1, PAIR_SWAP)
        near1 = send(x1, MID_SWAP)
        o_cands = (w_out, o_in, o_near, o_far, o_one, o_two)
        places = (
            table(me, 0, 1, -1, -1),
            table(me, -1, 0, -1, -1),
            table(me, -1, -1, 1, -1),
            table(me, -1, -1, 0, -1),
            table(me, 1, -1, -1, 1),
            table(me, -1, -1, -1, 0),
        )
        o_starts = starts_of(o_rows, places)
        g0, gain_sum = backward(o_starts, normed_t, w0, cotangent, tab, kept0, gain_sum, o_cands)
        pair1, near1 = lax.optimization_barrier((pair1, near1, g0))[:2]
        far1 = send(pair1, MID_SWAP)
        end_near1 = send(near1, OUTWARD)
        grad0 = scatter_merged(g0, me)
        go_over0 = send(plus(go0, go_in0), [(2, 1)])
        far1, end_near1 = lax.optimization_barrier((far1, end_near1))
        end_far1 = send(far1, OUTWARD)
        o_three = send(after(jnp.where(me == 2, w_out, o_near), end_far1), OUTWARD)
        *kept1, go1, w1 = forward(
            after(q_starts, *synced), normed, cotangent, tab, (x1, pair1, near1, far1, end_near1, end_far1)
        )
        go1 = go1.reshape(2, o_rows, width)
        go_in1_far = send(go1[1:], [(0, 1)])
        go_in1_near = send(go1[:1], [(0, 1)])
        o_cands = (w_out, o_in, o_near, o_far, o_three, o_two)
        places = (
            table(me, -1, -1, 0, 1),
            table(me, -1, -1, 1, -1),
            table(me, -1, 0, -1, -1),
            table(me, -1, 1, -1, -1),
            table(me, 0, -1, -1, 0),
            table(me, 1, -1, -1, -1),
        )
        g1, gain_sum = backward(
            starts_of(o_rows, places), normed_t, w1, cotangent, tab, kept1, after(gain_sum, go1), o_cands
        )
    else:
        *kept1, go1, w1 = forward(q_starts, normed, cotangent, tab, q_cands[1])
        go = jnp.concatenate([go0, go1], axis=0)
        none = jnp.zeros((1,), jnp.int32)
        out_grad = (none, (lax.psum_scatter(go, "fsdp", scatter_dimension=0, tiled=True)[None],))
        grads = []
        for pair, kept, w in ((0, kept0, w0), (1, kept1, w1)):
            g, gain_sum = backward(
                q_starts, normed_t, w, cotangent, tab, kept, gain_sum, (all_out[pair * QP : (pair + 1) * QP],)
            )
            grads.append((none, (lax.psum_scatter(g, "fsdp", scatter_dimension=0, tiled=True)[None],)))

    def adam_pair(pair, grad, held):
        return qkv_adam(pair, grad, w_qkv, qkv_first[0], qkv_second[0], qkv_whole, held)

    if line:
        qkv_state = adam_pair(0, grad0, ())
        go_over1_far = send(plus(go1[1:], go_in1_far), [(1, 2)])
        go_over1_near = send(plus(go1[:1], go_in1_near), [(1, 2)])
        low = me < 2
        mine = jnp.where(low, go0, go1)
        over1 = jnp.concatenate([go_over1_near, go_over1_far], axis=0)
        over = jnp.where(low, go_over0, over1)
        odd = me & 1
        go_out = send(plus(block(mine, 1 - odd), block(over, 1 - odd)), PAIR_SWAP)
        out_grad = (jnp.stack([odd, odd, odd * 0]).astype(jnp.int32), (mine, over, go_out))
        out_state = out_adam(out_grad, w_out, out_first[0], out_second[0], out_whole)
        grad1 = scatter_single(g1, me, (qkv_state[0],))
    else:
        out_state = out_adam(out_grad, w_out, out_first[0], out_second[0], out_whole)
        qkv_state = adam_pair(0, grads[0], ())
        grad1 = grads[1]
    qkv_state = adam_pair(1, grad1, qkv_state)

    gain_grad = all_sum(gain_sum[0], "fsdp", n) / gain
    gain_step, gain_first_next, gain_second_next = adam(gain, gain_grad, gain_first[0], gain_second[0], 0.0)

    gain_next = MIXING * gain_step + (1.0 - MIXING) * gain_pair[0]
    return (
        gain_next[None],
        qkv_state[0][None],
        out_state[0][None],
        gain_first_next[None],
        gain_second_next[None],
        qkv_state[1][None],
        qkv_state[2][None],
        out_state[1][None],
        out_state[2][None],
        gain_pair[0],
        gain_pair[1],
        qkv_pair[0],
        qkv_pair[1],
        out_pair[0],
        out_pair[1],
    )


def solution(mesh):
    placed = (
        P(("island", "fsdp"), None),
        P(("island", "fsdp"), None),
        P("island", None),
        P("island", "fsdp", None),
        P("island", "fsdp", None),
        P("island", None),
        P("island", None),
        P("island", "fsdp", None),
        P("island", "fsdp", None),
        P("island", "fsdp", None),
        P("island", "fsdp", None),
        P(),
        P(),
        P("fsdp", "island"),
        P("fsdp", "island"),
        P("fsdp", "island"),
        P("fsdp", "island"),
    )
    return jax.shard_map(
        shards,
        mesh=mesh,
        in_specs=placed,
        out_specs=(
            P("island", None),
            P("island", "fsdp", None),
            P("island", "fsdp", None),
            P("island", None),
            P("island", None),
            P("island", "fsdp", None),
            P("island", "fsdp", None),
            P("island", "fsdp", None),
            P("island", "fsdp", None),
            P(),
            P(),
            P("fsdp", "island"),
            P("fsdp", "island"),
            P("fsdp", "island"),
            P("fsdp", "island"),
        ),
        check_vma=False,
    )
```

```python
import functools

import jax
import jax.numpy as jnp
from jax import lax
from jax.experimental import pallas as pl
from jax.experimental.pallas import tpu as pltpu
from jax.sharding import PartitionSpec as P

HEADS = 16
KV_HEADS = 4
HEAD_DIM = 64
GROUP = HEADS // KV_HEADS
QP = 2 * GROUP * HEAD_DIM
CP = QP + 4 * HEAD_DIM

BETA_ONE = 0.9
BETA_TWO = 0.95
ADAM_EPS = 1e-08
INNER_RATE = 0.001
WEIGHT_DECAY = 0.1
STEP_COUNT = 100.0
OUTER_RATE = 0.7
OUTER_MOMENTUM = 0.9
MIXING = 0.5
NORM_EPS = 1e-05
ROPE_BASE = 500000.0
VMEM_LIMIT = 50 * 1024 * 1024

PAIRS = KV_HEADS // 2
F32 = jnp.float32
BF16 = jnp.bfloat16
NN = (((1,), (0,)), ((), ()))
NT = (((1,), (1,)), ((), ()))


def mm(a, b, dims=NN):
    return lax.dot_general(a, b, dims, preferred_element_type=F32)


def rope_tables(length):
    half = HEAD_DIM // 2
    freqs = ROPE_BASE ** (-jnp.arange(half, dtype=F32) / half)
    angles = jnp.arange(length, dtype=F32)[:, None] * freqs[None, :]
    cosine = jnp.cos(angles)
    sine = jnp.sin(angles)
    zero = jnp.zeros_like(sine)
    c = jnp.concatenate([cosine] * 4, axis=1)
    above = jnp.concatenate([zero, sine] * 2, axis=1)
    below = jnp.concatenate([-sine, zero] * 2, axis=1)
    return jnp.stack([c, above, below])


def turn(x, tab, sign):
    side = pltpu.roll(x, 32, 1) * tab[1] + pltpu.roll(x, 96, 1) * tab[2]
    return x * tab[0] + sign * side


def halves(x, at):
    lane = lax.broadcasted_iota(jnp.int32, x.shape, 1)
    alone = jnp.where((lane < HEAD_DIM) == (at == 0), x, 0.0)
    other = pltpu.roll(alone, HEAD_DIM, 1)
    pair = (alone, other) if at == 0 else (other, alone)
    return tuple(t.astype(BF16) for t in pair)


def added(total, part):
    return part if total is None else total + part


def assemble(starts, cands, whole, sems):
    def copy_of(at):
        rows = cands[at].shape[0]
        to = pl.ds(pl.multiple_of(starts[at], rows), rows)
        return pltpu.make_async_copy(cands[at], whole.at[to], sems.at[at])

    for at in range(len(cands)):
        @pl.when(starts[at] >= 0)
        def _(at=at):
            copy_of(at).start()
    for at in range(len(cands)):
        @pl.when(starts[at] >= 0)
        def _(at=at):
            copy_of(at).wait()


def forward_kernel(n_cand, starts, normed, cot, tab, *refs):
    cands = refs[:n_cand]
    q_ref, k_ref, v_ref, top_ref, low_ref, go_ref, w_ref, sems = refs[n_cand:]

    assemble(starts, cands, w_ref, sems)
    length = normed.shape[0]
    step = length // 2
    x = normed[...]
    k_tile = turn(mm(x, w_ref[:, QP : QP + 128]), tab, 1.0).astype(BF16)
    v_tile = mm(x, w_ref[:, QP + 128 :]).astype(BF16)
    k_ref[...] = k_tile
    v_ref[...] = v_tile
    row = lax.broadcasted_iota(jnp.int32, (step, step), 0)
    col = lax.broadcasted_iota(jnp.int32, (step, step), 1)
    causal = row >= col
    for group in range(2):
        keys = halves(k_tile.astype(F32), group)
        values = halves(v_tile.astype(F32), group)
        for pair in range(GROUP // 2):
            tile = group * (GROUP // 2) + pair
            cut = slice(tile * 128, tile * 128 + 128)
            q = turn(mm(x, w_ref[:, cut]), tab, 1.0).astype(BF16).astype(F32) * HEAD_DIM**-0.5
            q = q.astype(BF16)
            q_ref[:, cut] = q
            att = [None] * 2
            for half in range(2):
                head = tile * 2 + half
                for blk in range(2):
                    r0 = blk * step
                    nk = r0 + step
                    s = mm(q[r0:nk], keys[half][:nk], NT)
                    last = jnp.where(causal, s[:, r0:], -1e30)
                    s = last if blk == 0 else jnp.concatenate([s[:, :r0], last], axis=1)
                    top = jnp.max(s, axis=1, keepdims=True)
                    e = jnp.exp(s - top)
                    p = (e * (1.0 / jnp.sum(e, axis=1, keepdims=True))).astype(BF16)
                    if blk == 0:
                        top_ref[head] = p
                    else:
                        low_ref[head] = p
                    att[blk] = added(att[blk], mm(p, values[half][:nk]))
            att = jnp.concatenate(att, axis=0).astype(BF16).astype(F32).T.astype(BF16)
            go_ref[cut, :] = mm(att, cot[...]).astype(BF16)


def backward_kernel(n_cand, starts, normed_t, w_ref, cot, tab, q_ref, k_ref, v_ref, top_ref, low_ref, gain_in, *refs):
    cands = refs[:n_cand]
    g_ref, gain_ref, wo, sems = refs[n_cand:]
    assemble(starts, cands, wo, sems)
    length = cot.shape[0]
    step = length // 2
    dm = []
    dks = []
    dvs = []
    for group in range(2):
        keys = halves(k_ref[...].astype(F32), group)
        values = halves(v_ref[...].astype(F32), group)
        dk_t = [[None] * 2 for _ in range(2)]
        dv_t = [[None] * 2 for _ in range(2)]
        for pair in range(GROUP // 2):
            tile = group * (GROUP // 2) + pair
            cut = slice(tile * 128, tile * 128 + 128)
            da_f = mm(cot[...], wo[cut, :], NT)
            da = da_f.astype(BF16)
            da_t = da.astype(F32).T.astype(BF16)
            q_t = q_ref[:, cut].astype(F32).T.astype(BF16)
            dq = [None] * 2
            for half in range(2):
                head = tile * 2 + half
                key = keys[half]
                value = values[half]
                for blk in range(2):
                    r0 = blk * step
                    nk = r0 + step
                    pb = top_ref[head] if blk == 0 else low_ref[head]
                    p = pb.astype(F32)
                    dp = mm(da[r0:nk], value[:nk], NT)
                    ds = (p * (dp - jnp.sum(p * dp, axis=1, keepdims=True))).astype(BF16)
                    dq[blk] = added(dq[blk], mm(ds, key[:nk]))
                    dv = mm(da_t[:, r0:nk], pb)
                    dk = mm(q_t[:, r0:nk], ds)
                    for kb in range(blk + 1):
                        part = slice(kb * step, kb * step + step)
                        dv_t[half][kb] = added(dv_t[half][kb], dv[:, part])
                        dk_t[half][kb] = added(dk_t[half][kb], dk[:, part])
            dq = jnp.concatenate(dq, axis=0) * HEAD_DIM**-0.5
            dm.append(turn(dq, tab, -1.0).astype(BF16))
        dks.append([dk_t[0][kb][:HEAD_DIM] + dk_t[1][kb][HEAD_DIM:] for kb in range(2)])
        dvs.append([dv_t[0][kb][:HEAD_DIM] + dv_t[1][kb][HEAD_DIM:] for kb in range(2)])

    def joined(parts):
        return jnp.concatenate(
            [jnp.concatenate([parts[0][kb], parts[1][kb]], axis=0).T for kb in range(2)], axis=0
        )

    dm.append(turn(joined(dks), tab, -1.0).astype(BF16))
    dm.append(joined(dvs).astype(BF16))
    dm = jnp.concatenate(dm, axis=1)
    ones = jnp.ones((8, CP), BF16)
    block = 512
    for at in range(g_ref.shape[0] // block):
        cut = slice(at * block, at * block + block)
        g = mm(normed_t[cut, :], dm)
        g_ref[cut, :] = g.astype(BF16)
        prod = g * w_ref[cut, :].astype(F32)
        high = prod.astype(BF16)
        low = (prod - high.astype(F32)).astype(BF16)
        gain_ref[:, cut] = gain_in[:, cut] + mm(ones, high, NT) + mm(ones, low, NT)


def vmem_call(kernel, outs, n_hbm=0, hbm_at=0, smem=0, scratch=()):
    whole = pl.BlockSpec(memory_space=pltpu.VMEM)

    def call(*args):
        specs = [whole] * len(args)
        for i in range(smem):
            specs[i] = pl.BlockSpec(memory_space=pltpu.SMEM)
        for i in range(hbm_at, hbm_at + n_hbm):
            specs[i] = pl.BlockSpec(memory_space=pl.ANY)
        return pl.pallas_call(
            kernel,
            out_shape=outs,
            grid=(1,),
            in_specs=specs,
            out_specs=tuple(whole for _ in outs),
            scratch_shapes=list(scratch),
            compiler_params=pltpu.CompilerParams(vmem_limit_bytes=VMEM_LIMIT),
            cost_estimate=pl.CostEstimate(flops=1, bytes_accessed=1, transcendentals=0),
        )(*args)

    return call


def forward(starts, normed, cot, tab, cands):
    length, width = normed.shape
    step = length // 2
    heads = 2 * GROUP
    outs = (
        jax.ShapeDtypeStruct((length, QP), BF16),
        jax.ShapeDtypeStruct((length, 128), BF16),
        jax.ShapeDtypeStruct((length, 128), BF16),
        jax.ShapeDtypeStruct((heads, step, step), BF16),
        jax.ShapeDtypeStruct((heads, step, length), BF16),
        jax.ShapeDtypeStruct((QP, width), BF16),
        jax.ShapeDtypeStruct((width, CP), BF16),
    )
    call = vmem_call(
        functools.partial(forward_kernel, len(cands)),
        outs,
        n_hbm=len(cands),
        hbm_at=4,
        smem=1,
        scratch=[pltpu.SemaphoreType.DMA((len(cands),))],
    )
    return call(starts, normed, cot, tab, *cands)


def backward(starts, normed_t, w, cot, tab, saved, gain_in, cands):
    width = w.shape[0]
    outs = (
        jax.ShapeDtypeStruct((width, CP), BF16),
        jax.ShapeDtypeStruct((8, width), F32),
    )
    call = vmem_call(
        functools.partial(backward_kernel, len(cands)),
        outs,
        n_hbm=len(cands),
        hbm_at=6 + len(saved),
        smem=1,
        scratch=[pltpu.VMEM((QP, width), BF16), pltpu.SemaphoreType.DMA((len(cands),))],
    )
    return call(starts, normed_t, w, cot, tab, *saved, gain_in, *cands)


def norm_kernel(x_ref, gain_ref, out_ref, out_t_ref):
    block = 128
    for at in range(x_ref.shape[0] // block):
        cut = slice(at * block, at * block + block)
        x = x_ref[cut, :].astype(F32)
        factor = lax.rsqrt(jnp.mean(x * x, axis=1, keepdims=True) + NORM_EPS)
        y = (x * factor * gain_ref[...]).astype(BF16)
        out_ref[cut, :] = y
        out_t_ref[:, cut] = y.astype(F32).T.astype(BF16)


def norm(tokens, gain):
    length, width = tokens.shape
    outs = (jax.ShapeDtypeStruct((length, width), BF16), jax.ShapeDtypeStruct((width, length), BF16))
    return vmem_call(norm_kernel, outs)(tokens, gain)


def adam(wide, grad, first, second, decay):
    first_next = BETA_ONE * first + (1.0 - BETA_ONE) * grad
    second_next = BETA_TWO * second + (1.0 - BETA_TWO) * grad * grad
    update = (
        first_next
        / (1.0 - BETA_ONE**STEP_COUNT)
        / (jnp.sqrt(second_next / (1.0 - BETA_TWO**STEP_COUNT)) + ADAM_EPS)
    )
    return (wide - INNER_RATE * (update + decay * wide), first_next, second_next)


def mixed_step(w, grad, first, second, outer):
    stepped, first_next, second_next = adam(w.astype(F32), grad, first, second, WEIGHT_DECAY)
    new = (MIXING * stepped + (1.0 - MIXING) * outer.astype(F32)).astype(BF16)
    return new, first_next, second_next


def adam_kernel(n_parts, held, idx_ref, *refs):
    grad = refs[0][0].astype(F32)
    for part in refs[1:n_parts]:
        grad = grad + part[0].astype(F32)
    w, first, second, outer = refs[n_parts : n_parts + 4]
    new, first_next, second_next = refs[n_parts + 4 + held :]
    new[...], first_next[...], second_next[...] = mixed_step(
        w[...], grad, first[...], second[...], outer[...]
    )


def adam_call(grid, block, part_at, full_at, idx, parts, w, first, second, outer, held):
    rows, width = w.shape

    def part_spec(at):
        return pl.BlockSpec((1,) + block, lambda j, idx: (idx[at],) + part_at(j))

    full = pl.BlockSpec(block, lambda j, idx: full_at(j))
    n_parts = len(parts)
    return pl.pallas_call(
        functools.partial(adam_kernel, n_parts, len(held)),
        out_shape=(
            jax.ShapeDtypeStruct((rows, width), BF16),
            jax.ShapeDtypeStruct((rows, width), F32),
            jax.ShapeDtypeStruct((rows, width), F32),
        ),
        grid_spec=pltpu.PrefetchScalarGridSpec(
            num_scalar_prefetch=1,
            grid=(grid,),
            in_specs=[part_spec(i) for i in range(n_parts)]
            + [full] * 4
            + [pl.BlockSpec(memory_space=pl.ANY)] * len(held),
            out_specs=(full, full, full),
        ),
        input_output_aliases={1 + n_parts + 4 + i: i for i in range(len(held))},
        compiler_params=pltpu.CompilerParams(vmem_limit_bytes=VMEM_LIMIT),
        cost_estimate=pl.CostEstimate(flops=20_000_000, bytes_accessed=14_000_000, transcendentals=0),
    )(idx, *parts, w, first, second, outer, *held)


def qkv_adam(pair, grad, w, first, second, outer, held):
    q_blocks = QP // 128
    first_k = HEADS * HEAD_DIM // 128
    first_v = first_k + KV_HEADS * HEAD_DIM // 128

    def column(j):
        return (0, jnp.where(j < q_blocks, pair * q_blocks + j, jnp.where(j == q_blocks, first_k, first_v) + pair))

    idx, parts = grad
    return adam_call(
        CP // 128, (w.shape[0], 128), lambda j: (0, j), column, idx, parts, w, first, second, outer, held
    )


def out_adam(grad, w, first, second, outer):
    rows, width = w.shape
    idx, parts = grad
    return adam_call(
        rows // 64, (64, width), lambda j: (j, 0), lambda j: (j, 0), idx, parts, w, first, second, outer, ()
    )


def nesterov(global_value, momentum, average):
    delta = global_value - average
    momentum_next = OUTER_MOMENTUM * momentum + delta
    return (global_value - OUTER_RATE * (delta + OUTER_MOMENTUM * momentum_next), momentum_next)


def after(x, *others):
    return lax.optimization_barrier((x, *others))[0]


PAIR_SWAP = [(0, 1), (1, 0), (2, 3), (3, 2)]
MID_SWAP = [(1, 2), (2, 1)]
INWARD = [(0, 1), (3, 2)]
OUTWARD = [(1, 0), (2, 3)]


def send(x, pairs):
    return lax.ppermute(x, "fsdp", pairs)


def table(me, *values):
    return jnp.array(values, jnp.int32)[me]


def plus(a, b):
    return (a.astype(F32) + b.astype(F32)).astype(BF16)


def block(x, at):
    return lax.dynamic_slice_in_dim(x, at, 1, 0)


def starts_of(rows, places):
    return jnp.stack([jnp.where(p < 0, -1, p * rows) for p in places]).astype(jnp.int32)


def line_starts(me, rows):
    return starts_of(
        rows,
        (
            me,
            me ^ 1,
            table(me, -1, 2, 1, -1),
            table(me, -1, 3, 0, -1),
            table(me, 2, -1, -1, 1),
            table(me, 3, -1, -1, 0),
        ),
    )


def scatter_merged(x, me):
    blocks = x.reshape(4, x.shape[0] // 4, x.shape[1])

    def two(at):
        return lax.dynamic_slice_in_dim(blocks, at, 2, 0)

    inward = send(two(table(me, 2, 0, 0, 0)), INWARD)
    across = send(plus(two(table(me, 0, 2, 0, 0)), inward), MID_SWAP)
    outward = send(plus(block(blocks, me ^ 1), block(across, table(me, 0, 0, 1, 0))), PAIR_SWAP)
    idx = jnp.stack([me, table(me, 0, 1, 0, 0), me * 0]).astype(jnp.int32)
    return idx, (blocks, across, outward)


def scatter_single(x, me, before):
    blocks = x.reshape(4, x.shape[0] // 4, x.shape[1])
    far_in = send(block(blocks, 3 - me), INWARD)
    near_in = send(block(blocks, table(me, 2, 0, 0, 1)), INWARD)
    far = send(plus(block(blocks, table(me, 0, 3, 0, 0)), far_in), MID_SWAP)
    near = send(plus(block(blocks, 3 - me), near_in), MID_SWAP)
    outward = send(after(plus(block(blocks, me ^ 1), far), *before), PAIR_SWAP)
    idx = jnp.stack([me, me * 0, me * 0]).astype(jnp.int32)
    return idx, (blocks, near, outward)


def all_sum(x, axis, n):
    k = 1
    while k < n:
        x = x + lax.ppermute(x, axis, [(i, i ^ k) for i in range(n)])
        k *= 2
    return x


def shards(
    tokens,
    cotangent,
    norm_gain,
    qkv_weight,
    out_weight,
    gain_first,
    gain_second,
    qkv_first,
    qkv_second,
    out_first,
    out_second,
    gain_global,
    gain_momentum,
    qkv_global,
    qkv_momentum,
    out_global,
    out_momentum,
):
    n = lax.axis_size("fsdp")
    islands = lax.axis_size("island")
    gain = norm_gain[0]
    w_qkv = qkv_weight[0]
    w_out = out_weight[0]
    length, width = tokens.shape

    me = lax.axis_index("fsdp")
    qw = HEADS * HEAD_DIM
    kw = KV_HEADS * HEAD_DIM

    packed = [
        jnp.concatenate(
            [
                w_qkv[:, pair * QP : (pair + 1) * QP],
                w_qkv[:, qw + pair * 128 : qw + (pair + 1) * 128],
                w_qkv[:, qw + kw + pair * 128 : qw + kw + (pair + 1) * 128],
            ],
            axis=1,
        )
        for pair in range(PAIRS)
    ]
    w_rows = w_qkv.shape[0]
    o_rows = w_out.shape[0]
    line = n == 4

    if line:
        x0, x1 = packed
        pair0 = send(x0, PAIR_SWAP)
        near0 = send(x0, MID_SWAP)
        normed, normed_t = norm(tokens, gain[None])
        tab = rope_tables(length)
        pair0, near0, normed, normed_t, tab, x1 = lax.optimization_barrier(
            (pair0, near0, normed, normed_t, tab, x1)
        )
        far0 = send(pair0, MID_SWAP)
        end_near0 = send(near0, OUTWARD)
        o_in = send(after(w_out, pair0, near0), INWARD)
        far0, end_near0 = lax.optimization_barrier((far0, end_near0))
        end_far0 = send(far0, OUTWARD)
        o_near = send(after(w_out, far0), MID_SWAP)
        end_far0, x1 = lax.optimization_barrier((end_far0, x1))
        pair1 = send(x1, PAIR_SWAP)
        near1 = send(x1, MID_SWAP)
        q_cands = [(x0, pair0, near0, far0, end_near0, end_far0)]
        q_starts = line_starts(me, w_rows)
    else:
        normed, normed_t = norm(tokens, gain[None])
        tab = rope_tables(length)
        q_cands = [(lax.all_gather(x, "fsdp", axis=0, tiled=True),) for x in packed]
        q_starts = starts_of(0, (me,))
        all_out = lax.all_gather(w_out, "fsdp", axis=0, tiled=True)

    scale = 1.0 / islands
    qkv_total = lax.psum_scatter(w_qkv, "island", scatter_dimension=1, tiled=True)
    out_total = lax.psum_scatter(w_out, "island", scatter_dimension=1, tiled=True)
    gain_total = all_sum(gain, "island", islands)
    gain_pair = nesterov(gain_global, gain_momentum, gain_total * scale)

    def outer(qkv_total, out_total):
        qkv_pair = nesterov(qkv_global, qkv_momentum, qkv_total.astype(F32) * scale)
        out_pair = nesterov(out_global, out_momentum, out_total.astype(F32) * scale)
        qkv_whole = lax.all_gather(qkv_pair[0].astype(BF16), "island", axis=1, tiled=True)
        out_whole = lax.all_gather(out_pair[0].astype(BF16), "island", axis=1, tiled=True)
        return qkv_pair, out_pair, qkv_whole, out_whole

    *kept0, go0, w0 = forward(q_starts, normed, cotangent, tab, q_cands[0])
    gain_sum = jnp.zeros((8, width), F32)
    if line:
        go0 = go0.reshape(2, o_rows, width)
        pair1, near1, go0 = lax.optimization_barrier((pair1, near1, go0))
        far1 = send(pair1, MID_SWAP)
        end_near1 = send(near1, OUTWARD)
        go_in0 = send(go0, [(3, 2)])
        go_last0 = send(go0[1:], [(0, 1)])
        far1, end_near1 = lax.optimization_barrier((far1, end_near1))
        end_far1 = send(far1, OUTWARD)
        o_far = send(after(o_in, far1), MID_SWAP)
        o_first = jnp.where(me == 1, w_out, o_near)
        end_far1, o_far, o_first = lax.optimization_barrier((end_far1, o_far, o_first))
        o_one = send(o_first, OUTWARD)
        o_two = send(o_far, OUTWARD)
        go_sum0 = plus(go0, go_in0)
        go_over0 = send(go_sum0, [(2, 1)])
        *kept1, go1, w1 = forward(
            after(q_starts, go_sum0),
            normed,
            cotangent,
            tab,
            (x1, pair1, near1, far1, end_near1, end_far1),
        )
        go1 = go1.reshape(2, o_rows, width)
        go_in1_far = send(go1[1:], [(0, 1)])
        go_in1_near = send(go1[:1], [(0, 1)])
        go_last1 = send(go1[:1], [(3, 2)])
        o_three = send(after(jnp.where(me == 2, w_out, o_near), go1), OUTWARD)
        places = (
            table(me, 0, 1, -1, -1),
            table(me, -1, 0, -1, -1),
            table(me, -1, -1, 1, -1),
            table(me, -1, -1, 0, -1),
            table(me, 1, -1, -1, 1),
            table(me, -1, -1, -1, 0),
        )
        g0, gain_sum = backward(
            starts_of(o_rows, places),
            normed_t,
            w0,
            cotangent,
            tab,
            kept0,
            after(gain_sum, go1),
            (w_out, o_in, o_near, o_far, o_one, o_two),
        )
        g0, go0, go1, qkv_total, out_total = lax.optimization_barrier((g0, go0, go1, qkv_total, out_total))
        qkv_pair, out_pair, qkv_whole, out_whole = outer(qkv_total, out_total)
        synced = (qkv_pair[0], qkv_pair[1], out_pair[0], out_pair[1])
        go_sum0 = plus(go0[:1], go_over0[:1])
        go_end0 = send(go_sum0, [(1, 0)])
        go_sum1_far = plus(go1[1:], go_in1_far)
        go_over1_far = send(go_sum1_far, [(1, 2)])
        go_sum1_near = plus(go1[:1], go_in1_near)
        grad0 = scatter_merged(g0, me)
        places = (
            table(me, -1, -1, 0, 1),
            table(me, -1, -1, 1, -1),
            table(me, -1, 0, -1, -1),
            table(me, -1, 1, -1, -1),
            table(me, 0, -1, -1, 0),
            table(me, 1, -1, -1, -1),
        )
        g1, gain_sum = backward(
            starts_of(o_rows, places),
            normed_t,
            w1,
            cotangent,
            tab,
            kept1,
            after(gain_sum, go_last0, go_last1, go_sum0, go_sum1_far, go_sum1_near, *synced),
            (w_out, o_in, o_near, o_far, o_three, o_two),
        )
    else:
        qkv_pair, out_pair, qkv_whole, out_whole = outer(qkv_total, out_total)
        *kept1, go1, w1 = forward(q_starts, normed, cotangent, tab, q_cands[1])
        go = jnp.concatenate([go0, go1], axis=0)
        none = jnp.zeros((1,), jnp.int32)
        out_grad = (none, (lax.psum_scatter(go, "fsdp", scatter_dimension=0, tiled=True)[None],))
        grads = []
        for pair, kept, w in ((0, kept0, w0), (1, kept1, w1)):
            g, gain_sum = backward(
                q_starts, normed_t, w, cotangent, tab, kept, gain_sum, (all_out[pair * QP : (pair + 1) * QP],)
            )
            grads.append((none, (lax.psum_scatter(g, "fsdp", scatter_dimension=0, tiled=True)[None],)))

    def adam_pair(pair, grad, held):
        return qkv_adam(pair, grad, w_qkv, qkv_first[0], qkv_second[0], qkv_whole, held)

    if line:
        qkv_state = adam_pair(0, grad0, ())
        go_over1_near = send(go_sum1_near, [(1, 2)])
        go_end1 = send(plus(go1[1:], go_over1_far), [(2, 3)])
        odd = me & 1
        mine = jnp.where(me < 2, go0, go1)
        none = me * 0
        out_grad = (
            jnp.stack([odd, odd] + [none] * 5).astype(jnp.int32),
            (mine, go_over0, go_over1_near, go_last0, go_last1, go_end0, go_end1),
        )
        out_state = out_adam(out_grad, w_out, out_first[0], out_second[0], out_whole)
        grad1 = scatter_single(g1, me, (qkv_state[0],))
    else:
        out_state = out_adam(out_grad, w_out, out_first[0], out_second[0], out_whole)
        qkv_state = adam_pair(0, grads[0], ())
        grad1 = grads[1]
    qkv_state = adam_pair(1, grad1, qkv_state)

    gain_grad = all_sum(gain_sum[0], "fsdp", n) / gain
    gain_step, gain_first_next, gain_second_next = adam(gain, gain_grad, gain_first[0], gain_second[0], 0.0)

    gain_next = MIXING * gain_step + (1.0 - MIXING) * gain_pair[0]
    return (
        gain_next[None],
        qkv_state[0][None],
        out_state[0][None],
        gain_first_next[None],
        gain_second_next[None],
        qkv_state[1][None],
        qkv_state[2][None],
        out_state[1][None],
        out_state[2][None],
        gain_pair[0],
        gain_pair[1],
        qkv_pair[0],
        qkv_pair[1],
        out_pair[0],
        out_pair[1],
    )


def solution(mesh):
    placed = (
        P(("island", "fsdp"), None),
        P(("island", "fsdp"), None),
        P("island", None),
        P("island", "fsdp", None),
        P("island", "fsdp", None),
        P("island", None),
        P("island", None),
        P("island", "fsdp", None),
        P("island", "fsdp", None),
        P("island", "fsdp", None),
        P("island", "fsdp", None),
        P(),
        P(),
        P("fsdp", "island"),
        P("fsdp", "island"),
        P("fsdp", "island"),
        P("fsdp", "island"),
    )
    return jax.shard_map(
        shards,
        mesh=mesh,
        in_specs=placed,
        out_specs=(
            P("island", None),
            P("island", "fsdp", None),
            P("island", "fsdp", None),
            P("island", None),
            P("island", None),
            P("island", "fsdp", None),
            P("island", "fsdp", None),
            P("island", "fsdp", None),
            P("island", "fsdp", None),
            P(),
            P(),
            P("fsdp", "island"),
            P("fsdp", "island"),
            P("fsdp", "island"),
            P("fsdp", "island"),
        ),
        check_vma=False,
    )
```
